512 devices in a mesh: dp: 128 (over z, y, core), section: 4 (over x).
Axes of the slice: x: 4, y: 4, z: 16, core: 2. Of those that a mesh axis runs over, the one named last changes fastest.
Arguments:
- frames: bfloat16 [768, 128, 1280], P('dp'), may hold values from -300 to 300
- block_utt: int32 [768], replicated, may hold values from -1 to 767, as said below
- block_dest: int32 [768], replicated, may hold values from -1 to 511, as said below
- ln_gain: float32 [1280], replicated, may hold values from 0.5 to 1.5
- ln_shift: float32 [1280], replicated, may hold values from -3 to 3
- w_qkv: bfloat16 [3, 1280, 1280], P(None, 'dp', 'section'), may hold values from -10 to 10
- w_out: bfloat16 [1280, 1280], P('section', 'dp'), may hold values from -0.15625 to 0.15625
- post_gain: float32 [1280], replicated, may hold values from 0.5 to 1.5
- post_shift: float32 [1280], replicated, may hold values from -3 to 3
- w_proj: bfloat16 [1280, 4096], P('dp', 'section'), may hold values from -0.15625 to 0.15625
- proj_bias: float32 [4096], P('section'), may hold values from -3 to 3
Outputs:
- lm_rows: bfloat16 [32768, 4096], P(('dp', 'section'))
The draws below stay inside these ranges and needn't reach their ends.
Inputs may be any that keep to these rules, and one draw needn't show every extreme that they name: `block_utt`: -1 marks an empty slot; equal values mark the blocks of one utterance, which lie on one device of dp and share one destination device. `block_dest`: -1 exactly where block_utt is -1; otherwise a device of dp times 4 plus a slot; the device is the block's own or one beside it; no two blocks name the same slot; at most 1 block of one device go to each neighbouring device, and on some device exactly 1 go each way.
All inputs are finite; a program needn't handle non-finite values.
Results may differ from the reference program's by a relative error of at most 0.012.
Values may be sent and summed in bfloat16 or wider, within the bound.
No kernel may reach another device: no remote copies, remote signals or barrier semaphores. Data moves between devices by JAX's collectives and lax.ppermute only.
A program may use at most 64 MiB of HBM per device.

```python
import math
from functools import partial
import jax
import jax.numpy as jnp
from jax import lax

D = 1280
HEADS = 20
LMW = 4096
FRAME_BLK = 128
SEND = 1
CAP = 4
BLK_IN = 6
HEAD = 64
BLOCKS_IN = 768
SLOTS = 512
LM_ROWS = 32768
N_DP = 128
N_SECTION = 4


def routing_tables(key):
    devices = BLOCKS_IN // BLK_IN
    subkeys = jax.random.split(key, 8)
    places = jnp.arange(devices, dtype=jnp.int32)
    leftward = jax.random.randint(subkeys[0], (devices,), 0, SEND + 1)
    rightward = jax.random.randint(subkeys[1], (devices,), 0, SEND + 1)
    chosen = jax.random.randint(subkeys[2], (), 1, devices - 1)
    leftward = jnp.where(places == chosen, SEND, leftward)
    rightward = jnp.where(places == chosen, SEND, rightward)
    leftward = jnp.where(places == 0, 0, leftward)
    rightward = jnp.where(places == devices - 1, 0, rightward)
    rightward = jnp.where(places == 0, SEND, rightward)
    leftward = jnp.where(places == devices - 1, SEND, leftward)
    spare = jax.random.randint(subkeys[3], (devices,), 0, SEND + 1)
    filled = jax.random.randint(subkeys[4], (), 0, devices)
    spare = jnp.where(places == filled, 0, spare)
    zero_one = jnp.zeros((1,), jnp.int32)
    from_lower = jnp.concatenate([zero_one, rightward[:-1]])
    from_upper = jnp.concatenate([leftward[1:], zero_one])
    staying = CAP - from_lower - from_upper - spare
    position = jnp.arange(BLK_IN, dtype=jnp.int32)[None, :]
    lead_count = leftward[:, None]
    stay_count = staying[:, None]
    trail_count = rightward[:, None]
    in_left = position < lead_count
    in_stay = (position >= lead_count) & (position < lead_count + stay_count)
    in_right = (position >= lead_count + stay_count) & (position < lead_count + stay_count + trail_count)
    offset = position - lead_count
    coins = jax.random.randint(subkeys[5], (devices, BLK_IN), 0, 2)
    breaks = in_stay & ((offset % 4 == 0) | (coins == 1))
    piece_start = lax.cummax(jnp.where(breaks, position, 0), axis=1)
    first_slot = places[:, None] * BLK_IN
    owner_ids = jnp.where(in_left, first_slot, jnp.where(in_stay, first_slot + piece_start, jnp.where(in_right, first_slot + lead_count + stay_count, -1)))
    scores = jax.random.randint(subkeys[6], (devices, CAP), 0, 2 ** 20) * CAP + jnp.arange(CAP, dtype=jnp.int32)[None, :]
    order_out = jnp.argsort(scores, axis=1, stable=True).astype(jnp.int32)
    stay_slot = jnp.take_along_axis(order_out, jnp.clip(offset, 0, CAP - 1), axis=1)
    upper_order = jnp.concatenate([order_out[1:], order_out[-1:]], axis=0)
    upper_stay = jnp.concatenate([staying[1:], zero_one])[:, None]
    right_index = jnp.clip(upper_stay + position - lead_count - stay_count, 0, CAP - 1)
    right_slot = jnp.take_along_axis(upper_order, right_index, axis=1)
    lower_order = jnp.concatenate([order_out[:1], order_out[:-1]], axis=0)
    lower_base = jnp.concatenate([zero_one, (staying + from_lower)[:-1]])[:, None]
    left_index = jnp.clip(lower_base + position, 0, CAP - 1)
    left_slot = jnp.take_along_axis(lower_order, left_index, axis=1)
    device_col = places[:, None]
    targets = jnp.where(in_left, (device_col - 1) * CAP + left_slot, jnp.where(in_stay, device_col * CAP + stay_slot, jnp.where(in_right, (device_col + 1) * CAP + right_slot, -1)))
    shuffle = jax.random.randint(subkeys[7], (devices, BLK_IN), 0, 2 ** 20) * BLK_IN + jnp.arange(BLK_IN, dtype=jnp.int32)[None, :]
    order_in = jnp.argsort(shuffle, axis=1, stable=True).astype(jnp.int32)
    owner_ids = jnp.take_along_axis(owner_ids, order_in, axis=1)
    targets = jnp.take_along_axis(targets, order_in, axis=1)
    return (owner_ids.reshape(-1).astype(jnp.int32), targets.reshape(-1).astype(jnp.int32))


def draw_block_utt(key, part):
    owner_ids, targets = routing_tables(key)
    return owner_ids


def draw_block_dest(key, part):
    owner_ids, targets = routing_tables(key)
    return targets


def draw_frames(key, part):
    key = jax.random.fold_in(key, 11)
    subkeys = jax.random.split(key, 1)
    noise = jnp.clip(jax.random.normal(subkeys[0], (BLOCKS_IN, FRAME_BLK, D), jnp.float32), -5.0, 5.0)
    return noise.astype(jnp.bfloat16)


def draw_w_qkv(key, part):
    key = jax.random.fold_in(key, 12)
    subkeys = jax.random.split(key, 1)
    base = jnp.clip(jax.random.normal(subkeys[0], (3, D, D), jnp.float32), -5.0, 5.0) / math.sqrt(D)
    return base.astype(jnp.bfloat16)


def level_of(rng, shape, pieces, low, top_value):
    def one(dim, blocks):
        heights = jax.random.uniform(jax.random.fold_in(jax.random.fold_in(rng, 6), dim), (blocks,), jnp.float32, low / len(pieces), top_value / len(pieces))
        return jnp.repeat(jnp.exp(heights), shape[dim] // blocks).reshape((-1,) + (1,) * (len(shape) - dim - 1))

    factor_of = one(*pieces[0])
    for cut in pieces[1:]:
        factor_of = factor_of * one(*cut)
    return factor_of


def scatter_about(stream_key, dims, width, reach, cuts=(), kind=jnp.bfloat16):
    result = width * jax.random.normal(stream_key, dims, jnp.float32)
    if cuts:
        result = result * level_of(stream_key, dims, cuts, -0.22, 0.18)
    return jnp.clip(result, -reach, reach).astype(kind)


def setup_inputs(seed: int = 0) -> dict:
    arg_keys = jax.random.split(jax.random.key(seed), 12)
    frames = draw_frames(jax.random.fold_in(arg_keys[11], 71), 0)
    block_utt = draw_block_utt(jax.random.fold_in(arg_keys[11], 71), 0)
    block_dest = draw_block_dest(jax.random.fold_in(arg_keys[11], 71), 0)
    ln_gain = jnp.clip(1.0 + 0.1 * jax.random.normal(arg_keys[3], (D,), jnp.float32), 0.5, 1.5)
    ln_shift = scatter_about(arg_keys[4], (D,), 0.5, 3.0, (), jnp.float32)
    w_qkv = draw_w_qkv(jax.random.fold_in(arg_keys[11], 71), 0)
    w_out = scatter_about(arg_keys[6], (D, D), D ** -0.5, 0.15625, ((0, 4), (1, 128)))
    post_gain = jnp.clip(1.0 + 0.1 * jax.random.normal(arg_keys[7], (D,), jnp.float32), 0.5, 1.5)
    post_shift = scatter_about(arg_keys[8], (D,), 0.5, 3.0, (), jnp.float32)
    w_proj = scatter_about(arg_keys[9], (D, LMW), D ** -0.5, 0.15625, ((0, 128), (1, 4)))
    proj_bias = scatter_about(arg_keys[10], (LMW,), 0.5, 3.0, ((0, 4),), jnp.float32)
    return dict(frames=frames, block_utt=block_utt, block_dest=block_dest, ln_gain=ln_gain, ln_shift=ln_shift, w_qkv=w_qkv, w_out=w_out, post_gain=post_gain, post_shift=post_shift, w_proj=w_proj, proj_bias=proj_bias)


def normalize(values, scale_gain, offset_term):
    centre = lax.optimization_barrier(jnp.mean(values, axis=-1, keepdims=True))
    centred = values - centre
    spread = lax.optimization_barrier(jnp.mean(centred * centred, axis=-1, keepdims=True))
    return centred * lax.rsqrt(spread + 1e-05) * scale_gain + offset_term

def attend_head(operands, same_owner):
    query, keyed, valued = operands
    scores = jnp.dot(query, keyed.T, preferred_element_type=jnp.float32) * HEAD ** (-0.5)
    scores = jnp.where(same_owner, scores, -1e+30)
    row_max = lax.optimization_barrier(jnp.max(scores, axis=1, keepdims=True))
    weights = jnp.exp(scores - row_max)
    weights = (weights / lax.optimization_barrier(jnp.sum(weights, axis=1, keepdims=True))).astype(jnp.bfloat16)
    return jnp.dot(weights, valued, preferred_element_type=jnp.float32).astype(jnp.bfloat16)

def reference(frames, block_utt, block_dest, ln_gain, ln_shift, w_qkv, w_out, post_gain, post_shift, w_proj, proj_bias):
    target_index = jnp.where(block_dest >= 0, block_dest, SLOTS).astype(jnp.int32)
    source = jnp.full((SLOTS + 1,), -1, jnp.int32).at[target_index].set(jnp.arange(BLOCKS_IN, dtype=jnp.int32))[:SLOTS]
    row_count = CAP * FRAME_BLK
    group_width = D // N_SECTION

    def encode_device(device):
        picked = lax.dynamic_slice_in_dim(source, (device * CAP).astype(jnp.int32), CAP)
        safe_pick = jnp.maximum(picked, 0)
        present = picked >= 0
        owners = jnp.where(present, block_utt[safe_pick], -1)
        blocks = jnp.where(present[:, None, None], frames[safe_pick], jnp.zeros((), frames.dtype))
        inputs = blocks.reshape(row_count, D).astype(jnp.float32)
        normed = normalize(inputs, ln_gain.astype(jnp.float32), ln_shift.astype(jnp.float32)).astype(jnp.bfloat16)
        projected_qkv = jnp.einsum('rd,tdc->trc', normed.astype(jnp.float32), w_qkv.astype(jnp.float32)).astype(jnp.bfloat16)
        split_heads = projected_qkv.reshape(3, row_count, HEADS, HEAD).transpose(0, 2, 1, 3)
        row_owner = jnp.repeat(owners, FRAME_BLK)
        same_owner = row_owner[:, None] == row_owner[None, :]
        heads_out = lax.map(partial(attend_head, same_owner=same_owner), (split_heads[0], split_heads[1], split_heads[2]))
        attended = heads_out.transpose(1, 0, 2).reshape(row_count, D)
        grouped = jnp.einsum('rgc,gcd->grd', attended.reshape(row_count, N_SECTION, group_width).astype(jnp.float32), w_out.reshape(N_SECTION, group_width, D).astype(jnp.float32))
        rounded = lax.optimization_barrier(grouped.astype(jnp.bfloat16))
        attention_sum = lax.optimization_barrier(jnp.sum(rounded.astype(jnp.float32), axis=0))
        resid = inputs + attention_sum
        pooled = resid.reshape(row_count // 2, 2, D).mean(axis=1)
        pooled_norm = normalize(pooled, post_gain.astype(jnp.float32), post_shift.astype(jnp.float32)).astype(jnp.bfloat16)
        lm_part = jnp.dot(pooled_norm, w_proj, preferred_element_type=jnp.float32) + proj_bias.astype(jnp.float32)
        live_rows = jnp.repeat(owners >= 0, FRAME_BLK // 2)
        return jnp.where(live_rows[:, None], lm_part, jnp.zeros((), jnp.float32)).astype(jnp.bfloat16)
    produced = lax.map(encode_device, jnp.arange(N_DP, dtype=jnp.int32))
    return produced.reshape(LM_ROWS, LMW)
```

```python
import functools

import jax
import jax.numpy as jnp
import numpy as np
from jax import lax
from jax.experimental import pallas as pl
from jax.experimental.pallas import tpu as pltpu
from jax.sharding import Mesh, PartitionSpec as P

CAP = 4
BLK_IN = 6
FRAMES = 128
D = 1280
HEAD = 64
PART = 320
PROJ = 1024
NY = 4
NC = 2
K_DEV = 10
TILES = 18
PACKED = 192
SLAB = 160
HALF = FRAMES // 2
POOLED = CAP * HALF
ROWS = CAP * FRAMES
EPS = 1e-05
NEG = -1e30
F32 = jnp.float32
BF16 = jnp.bfloat16
DP = ("z", "y", "core")
MIB = 1024 * 1024

VMEM = functools.partial(pl.BlockSpec, memory_space=pltpu.VMEM)
SMEM = functools.partial(pl.BlockSpec, memory_space=pltpu.SMEM)
ANY = functools.partial(pl.BlockSpec, memory_space=pl.ANY)

NT = (((1,), (1,)), ((), ()))


def dp_index():
    return (lax.axis_index("z") * NY + lax.axis_index("y")) * NC + lax.axis_index("core")


def feature_order(nz):
    order = np.arange(D).reshape(nz, NY * NC, K_DEV).transpose(1, 0, 2).reshape(1, D)
    return jnp.asarray(order, jnp.int32)


def plan_kernel(utt, dest, frames, wq, wo, wp, plan, down, up, packed, stage, sems):
    device = dp_index()
    last = dest.shape[0] // BLK_IN - 1
    base = device * BLK_IN
    to_down = jnp.int32(0)
    to_up = jnp.int32(0)
    for g in range(CAP):
        plan[g] = -1
        plan[CAP + g] = -1

    def take(position, code):
        target = dest[position]

        @pl.when((target >= 0) & (target // CAP == device))
        def _():
            slot = target % CAP
            plan[slot] = code
            plan[CAP + slot] = utt[position]

        return target

    for j in range(BLK_IN):
        target = take(base + j, j)
        owner = jnp.where(target >= 0, target // CAP, -9)
        to_down = jnp.where(owner == device - 1, j, to_down)
        to_up = jnp.where(owner == device + 1, j, to_up)
    down_copy = pltpu.make_async_copy(frames.at[to_down], down, sems.at[0])
    up_copy = pltpu.make_async_copy(frames.at[to_up], up, sems.at[1])
    down_copy.start()
    up_copy.start()
    for j in range(BLK_IN):

        @pl.when(device > 0)
        def _():
            take(base - BLK_IN + j, BLK_IN)

        @pl.when(device < last)
        def _():
            take(base + BLK_IN + j, BLK_IN + 1)

    rows = lax.broadcasted_iota(jnp.int32, (K_DEV, K_DEV), 0)
    cols = lax.broadcasted_iota(jnp.int32, (K_DEV, K_DEV), 1)
    eye = jnp.where(rows == cols, 1.0, 0.0).astype(BF16)
    w_out = lax.dot_general(eye, wo[...], NT, preferred_element_type=F32)
    parts = [wq[0].astype(F32), wq[1].astype(F32), wq[2].astype(F32), w_out]
    tiles = []
    for part in parts:
        tiles += [part[:, :128], part[:, 128:256]]
    tails = [part[:, 256:320] for part in parts]
    tiles.append(jnp.concatenate(tails[:2], axis=1))
    tiles.append(jnp.concatenate(tails[2:], axis=1))
    proj = wp[...].astype(F32)
    tiles += [proj[:, i * 128 : (i + 1) * 128] for i in range(PROJ // 128)]
    for i, tile in enumerate(tiles):
        stage[i * K_DEV : (i + 1) * K_DEV, :] = tile
    used = TILES * K_DEV
    stage[used:, :] = jnp.zeros((PACKED - used, 128), F32)
    packed[...] = stage[...].astype(BF16)
    down_copy.wait()
    up_copy.wait()


def plan_call(block_utt, block_dest, frames, w_qkv, w_out, w_proj):
    block = jax.ShapeDtypeStruct((FRAMES, D), BF16)
    return pl.pallas_call(
        plan_kernel,
        out_shape=(
            jax.ShapeDtypeStruct((2 * CAP,), jnp.int32),
            block,
            block,
            jax.ShapeDtypeStruct((PACKED, 128), BF16),
        ),
        in_specs=[SMEM(), SMEM(), ANY(), VMEM(), VMEM(), VMEM()],
        out_specs=(SMEM(), ANY(), ANY(), VMEM()),
        scratch_shapes=[pltpu.VMEM((PACKED, 128), F32), pltpu.SemaphoreType.DMA((2,))],
        name="plan",
    )(block_utt, block_dest, frames, w_qkv, w_out, w_proj)


def unpack_kernel(gathered, main, proj, flat, stage):
    nz = gathered.shape[0] // PACKED
    for z in range(nz):
        flat[...] = gathered[z * PACKED : (z + 1) * PACKED, :].astype(F32)
        for i in range(TILES):
            stage[z * K_DEV : (z + 1) * K_DEV, i * 128 : (i + 1) * 128] = flat[
                i * K_DEV : (i + 1) * K_DEV, :
            ]
    main[...] = stage[:, :D].astype(BF16)
    proj[...] = stage[:, D:].astype(BF16)


def unpack_call(gathered):
    slab = gathered.shape[0] // PACKED * K_DEV
    return pl.pallas_call(
        unpack_kernel,
        out_shape=(
            jax.ShapeDtypeStruct((slab, D), BF16),
            jax.ShapeDtypeStruct((slab, PROJ), BF16),
        ),
        in_specs=[VMEM()],
        out_specs=(VMEM(), VMEM()),
        scratch_shapes=[
            pltpu.VMEM((PACKED, 128), F32),
            pltpu.VMEM((slab, D + PROJ), F32),
        ],
        compiler_params=pltpu.CompilerParams(vmem_limit_bytes=32 * MIB),
        cost_estimate=pl.CostEstimate(flops=0, bytes_accessed=2 * MIB, transcendentals=0),
        name="unpack",
    )(gathered)


def layer_norm(values, gain, shift):
    centre = jnp.mean(values, axis=-1, keepdims=True)
    centred = values - centre
    spread = jnp.mean(centred * centred, axis=-1, keepdims=True)
    return centred * lax.rsqrt(spread + EPS) * gain + shift


def split_exact(values):
    high = values.astype(BF16)
    rest = values - high.astype(F32)
    middle = rest.astype(BF16)
    low = (rest - middle.astype(F32)).astype(BF16)
    return [high, middle, low]


def prepare_kernel(
    plan, frames, from_lower, from_upper, gain, shift, post_gain, post_shift, order,
    normed, residual, post, blocks, stack, sems,
):
    for g in range(CAP):
        source = plan[g]

        @pl.when((source >= 0) & (source < BLK_IN))
        def _():
            pltpu.make_async_copy(frames.at[source], blocks.at[g], sems.at[g]).start()

        @pl.when(source == BLK_IN)
        def _():
            pltpu.make_async_copy(from_lower, blocks.at[g], sems.at[g]).start()

        @pl.when(source == BLK_IN + 1)
        def _():
            pltpu.make_async_copy(from_upper, blocks.at[g], sems.at[g]).start()

        @pl.when(source < 0)
        def _():
            blocks[g] = jnp.zeros((FRAMES, D), BF16)

    parts = split_exact(post_gain[...]) + split_exact(post_shift[...])
    stack[ROWS + FRAMES :, :] = jnp.concatenate(
        parts + [jnp.zeros((10, D), BF16)], axis=0
    )
    for g in range(CAP):

        @pl.when(plan[g] >= 0)
        def _():
            pltpu.make_async_copy(from_lower, blocks.at[g], sems.at[g]).wait()

    rows = lax.broadcasted_iota(jnp.int32, (FRAMES, FRAMES), 0)
    cols = lax.broadcasted_iota(jnp.int32, (FRAMES, FRAMES), 1)
    picked = jnp.where(rows < HALF, 2 * rows, 2 * (rows - HALF) + 1)
    parity = jnp.where(cols == picked, 1.0, 0.0).astype(BF16)
    for g in range(CAP):
        sorted_rows = jnp.dot(parity, blocks[g], preferred_element_type=F32)
        done = layer_norm(sorted_rows, gain[...], shift[...]).astype(BF16)
        stack[g * HALF : (g + 1) * HALF, :] = done[:HALF]
        stack[POOLED + g * HALF : POOLED + (g + 1) * HALF, :] = done[HALF:]
    own = blocks[lax.axis_index("section")]
    stack[ROWS : ROWS + FRAMES, :] = jnp.dot(
        parity, own, preferred_element_type=F32
    ).astype(BF16)
    for start in range(0, D, 256):
        feature = lax.broadcasted_iota(jnp.int32, (D, 256), 0)
        wanted = order[:, start : start + 256]
        select = jnp.where(feature == wanted, 1.0, 0.0).astype(BF16)
        moved = jnp.dot(stack[...], select, preferred_element_type=F32)
        span = slice(start, start + 256)
        normed[:, span] = moved[:ROWS].astype(BF16)
        residual[:, span] = 0.5 * (
            moved[ROWS : ROWS + HALF] + moved[ROWS + HALF : ROWS + FRAMES]
        )
        tail = moved[ROWS + FRAMES :]
        post[0:1, span] = tail[0:1] + (tail[1:2] + tail[2:3])
        post[1:2, span] = tail[3:4] + (tail[4:5] + tail[5:6])


def prepare_call(plan, frames, from_lower, from_upper, vectors, order):
    return pl.pallas_call(
        prepare_kernel,
        out_shape=(
            jax.ShapeDtypeStruct((ROWS, D), BF16),
            jax.ShapeDtypeStruct((HALF, D), F32),
            jax.ShapeDtypeStruct((2, D), F32),
        ),
        in_specs=[SMEM(), ANY(), ANY(), ANY()] + [VMEM()] * 5,
        out_specs=(VMEM(), VMEM(), VMEM()),
        scratch_shapes=[
            pltpu.VMEM((CAP, FRAMES, D), BF16),
            pltpu.VMEM((ROWS + FRAMES + 16, D), BF16),
            pltpu.SemaphoreType.DMA((CAP,)),
        ],
        compiler_params=pltpu.CompilerParams(vmem_limit_bytes=40 * MIB),
        cost_estimate=pl.CostEstimate(
            flops=4 * 656 * D * D, bytes_accessed=8 * MIB, transcendentals=0
        ),
        name="prepare",
    )(plan, frames, from_lower, from_upper, *vectors, order)


def attend_kernel(plan, normed, mine, other, terms, weights, sems):
    core = lax.axis_index("core")
    y = lax.axis_index("y")
    copies = []
    for i, (source, side) in enumerate(((mine, core), (other, 1 - core))):
        for r in range(NY):
            row = ((y + r) % NY * NC + side) * SLAB
            row = pl.multiple_of(row, 32)
            copies.append(
                pltpu.make_async_copy(
                    source.at[pl.ds(r * SLAB, SLAB)],
                    weights.at[pl.ds(row, SLAB)],
                    sems.at[i * NY + r],
                )
            )
    for copy in copies:
        copy.start()
    slot_row = lax.broadcasted_iota(jnp.int32, (ROWS, 1), 0) % POOLED // HALF
    slot_col = lax.broadcasted_iota(jnp.int32, (1, ROWS), 1) % POOLED // HALF
    owner_row = jnp.full((ROWS, 1), -1, jnp.int32)
    owner_col = jnp.full((1, ROWS), -1, jnp.int32)
    for g in range(CAP):
        owner = plan[CAP + g]
        owner_row = jnp.where(slot_row == g, owner, owner_row)
        owner_col = jnp.where(slot_col == g, owner, owner_col)
    same = owner_row == owner_col
    low = lax.broadcasted_iota(jnp.int32, (1, 128), 1) < HEAD
    for copy in copies:
        copy.wait()
    x = normed[...]

    def project(start, size):
        return jnp.dot(x, weights[:, start : start + size], preferred_element_type=F32)

    def head(query, keyed, valued, use_low):
        query = jnp.where(low == use_low, query, 0.0).astype(BF16)
        scores = lax.dot_general(query, keyed, NT, preferred_element_type=F32)
        scores = jnp.where(same, scores * HEAD ** (-0.5), NEG)
        peak = jnp.max(scores, axis=1, keepdims=True)
        weight = jnp.exp(scores - peak)
        total = jnp.sum(weight, axis=1, keepdims=True)
        weight = (weight / total).astype(BF16)
        out = jnp.dot(weight, valued, preferred_element_type=F32)
        return 0.5 * (out[:POOLED] + out[POOLED:])

    queries = project(0, 256)
    keys = project(256, 256).astype(BF16)
    values = project(512, 256).astype(BF16)
    tail = project(1024, 256)
    pieces = []
    for pair in range(2):
        span = slice(pair * 128, (pair + 1) * 128)
        query, keyed, valued = queries[:, span], keys[:, span], values[:, span]
        first = head(query, keyed, valued, True)
        second = head(query, keyed, valued, False)
        pieces.append(jnp.where(low, first, second).astype(BF16))
    pair = tail[:, :128]
    rolled = pltpu.roll(pair, HEAD, 1).astype(BF16)
    fifth = head(pair, rolled, tail[:, 128:].astype(BF16), True)
    fifth = pltpu.roll(fifth, HEAD, 1)
    fifth = jnp.where(low, 0.0, fifth).astype(BF16)
    pooled = jnp.concatenate(pieces + [fifth], axis=1)
    for start in range(0, D, 256):
        rows = slice(start, start + 256)
        out = lax.dot_general(
            pooled[:, :256], weights[rows, 768:1024], NT, preferred_element_type=F32
        ) + lax.dot_general(
            pooled[:, 256:], weights[rows, 1152:1280], NT, preferred_element_type=F32
        )
        terms[:, rows] = out.astype(BF16)


def attend_call(plan, normed, mine, other):
    return pl.pallas_call(
        attend_kernel,
        out_shape=jax.ShapeDtypeStruct((POOLED, D), BF16),
        in_specs=[SMEM(), VMEM(), ANY(), ANY()],
        out_specs=VMEM(),
        scratch_shapes=[
            pltpu.VMEM((D, D), BF16),
            pltpu.SemaphoreType.DMA((2 * NY,)),
        ],
        compiler_params=pltpu.CompilerParams(vmem_limit_bytes=48 * MIB),
        cost_estimate=pl.CostEstimate(
            flops=3 * 10**9, bytes_accessed=8 * MIB, transcendentals=5 * ROWS * ROWS
        ),
        name="attend",
    )(plan, normed, mine, other)


def finish_kernel(terms, residual, post, out):
    total = residual[...]
    for s in range(terms.shape[0] // HALF):
        total += terms[s * HALF : (s + 1) * HALF, :].astype(F32)
    out[...] = layer_norm(total, post[0:1, :], post[1:2, :]).astype(BF16)


def finish_call(terms, residual, post):
    return pl.pallas_call(
        finish_kernel,
        out_shape=jax.ShapeDtypeStruct((HALF, D), BF16),
        in_specs=[VMEM()] * 3,
        out_specs=VMEM(),
        compiler_params=pltpu.CompilerParams(vmem_limit_bytes=16 * MIB),
        name="finish",
    )(terms, residual, post)


def project_kernel(plan, rows, weights, bias, out):
    for g in range(CAP):
        span = slice(g * HALF, (g + 1) * HALF)
        value = jnp.dot(rows[span, :], weights[...], preferred_element_type=F32)
        value = value + bias[...]
        out[span, :] = jnp.where(plan[CAP + g] >= 0, value, 0.0).astype(BF16)


def project_call(plan, rows, weights, bias):
    return pl.pallas_call(
        project_kernel,
        out_shape=jax.ShapeDtypeStruct((POOLED, PROJ), BF16),
        in_specs=[SMEM(), VMEM(), VMEM(), VMEM()],
        out_specs=VMEM(),
        compiler_params=pltpu.CompilerParams(vmem_limit_bytes=32 * MIB),
        cost_estimate=pl.CostEstimate(
            flops=2 * POOLED * D * PROJ, bytes_accessed=4 * MIB, transcendentals=0
        ),
        name="project",
    )(plan, rows, weights, bias)


def shards(
    frames,
    block_utt,
    block_dest,
    ln_gain,
    ln_shift,
    w_qkv,
    w_out,
    post_gain,
    post_shift,
    w_proj,
    proj_bias,
):
    plan, down, up, packed = plan_call(
        block_utt, block_dest, frames, w_qkv, w_out, w_proj
    )
    up_ring = [(i, i + 1) for i in range(lax.axis_size(DP) - 1)]
    from_lower = lax.ppermute(up, DP, up_ring)
    from_upper = lax.ppermute(down, DP, [(j, i) for i, j in up_ring])
    gathered = lax.all_gather(packed, "z", axis=0, tiled=True)
    main, proj = unpack_call(gathered)
    proj_all = lax.all_gather(proj, ("y", "core"), axis=0, tiled=True)
    slabs = [main]
    for r in range(1, NY):
        ring = [((i + r) % NY, i) for i in range(NY)]
        slabs.append(lax.ppermute(main, "y", ring))
    mine = jnp.concatenate(slabs, axis=0)
    other = lax.ppermute(mine, "core", [(0, 1), (1, 0)])
    order = feature_order(lax.axis_size("z"))
    vectors = [v.reshape(1, D) for v in (ln_gain, ln_shift, post_gain, post_shift)]
    normed, residual, post = prepare_call(
        plan, frames, from_lower, from_upper, vectors, order
    )
    terms = attend_call(plan, normed, mine, other)
    terms = lax.all_to_all(terms, "section", split_axis=0, concat_axis=0, tiled=True)
    pooled_norm = finish_call(terms, residual, post)
    rows = lax.all_gather(pooled_norm, "section", axis=0, tiled=True)
    lm_local = project_call(plan, rows, proj_all, proj_bias.reshape(1, PROJ))
    return lax.all_to_all(lm_local, "section", split_axis=0, concat_axis=1, tiled=True)


def solution(mesh):
    dp, section = mesh.devices.shape
    shape = (dp // (NY * NC), NY, NC, section)
    fine = Mesh(mesh.devices.reshape(shape), DP + ("section",))
    return jax.shard_map(
        shards,
        mesh=fine,
        in_specs=(
            P(DP, None, None),
            P(),
            P(),
            P(),
            P(),
            P(None, DP, "section"),
            P("section", DP),
            P(),
            P(),
            P(DP, "section"),
            P("section"),
        ),
        out_specs=P(DP + ("section",), None),
        check_vma=False,
    )
```

```python
import functools

import jax
import jax.numpy as jnp
import numpy as np
from jax import lax
from jax.experimental import pallas as pl
from jax.experimental.pallas import tpu as pltpu
from jax.sharding import Mesh, PartitionSpec as P

CAP = 4
BLK_IN = 6
FRAMES = 128
D = 1280
HEAD = 64
PART = 320
PROJ = 1024
NY = 4
NC = 2
Y_ORDER = (0, 2, 1, 3)
K_DEV = 10
TILES = 18
PACKED = 192
SLAB = 160
HALF = FRAMES // 2
POOLED = CAP * HALF
ROWS = CAP * FRAMES
EPS = 1e-05
NEG = -1e30
F32 = jnp.float32
BF16 = jnp.bfloat16
DP = ("z", "y", "core")
MIB = 1024 * 1024
WIDE = 58 * MIB

VMEM = functools.partial(pl.BlockSpec, memory_space=pltpu.VMEM)
SMEM = functools.partial(pl.BlockSpec, memory_space=pltpu.SMEM)
ANY = functools.partial(pl.BlockSpec, memory_space=pl.ANY)

NT = (((1,), (1,)), ((), ()))


def dp_index():
    return (lax.axis_index("z") * NY + lax.axis_index("y")) * NC + lax.axis_index("core")


def feature_order(nz):
    order = np.arange(D).reshape(nz, NY * NC, K_DEV).transpose(1, 0, 2).reshape(1, D)
    return jnp.asarray(order, jnp.int32)


def plan_kernel(utt, dest, frames, wq, wo, wp, plan, packed, far, stage, sem):
    core = lax.axis_index("core")
    device = dp_index()
    last = dest.shape[0] // BLK_IN - 1
    base = device * BLK_IN
    to_down = jnp.int32(0)
    to_up = jnp.int32(0)
    from_lower = BLK_IN + core
    from_upper = BLK_IN + 1 - core
    for g in range(2 * CAP):
        plan[g] = -1

    def take(position, code):
        target = dest[position]

        @pl.when((target >= 0) & (target // CAP == device))
        def _():
            slot = target % CAP
            plan[slot] = code
            plan[CAP + slot] = utt[position]

        return target

    for j in range(BLK_IN):
        target = take(base + j, j)
        owner = jnp.where(target >= 0, target // CAP, -9)
        to_down = jnp.where(owner == device - 1, j, to_down)
        to_up = jnp.where(owner == device + 1, j, to_up)
    leaving = jnp.where(core == 0, to_down, to_up)
    plan[2 * CAP] = jnp.where(core == 0, to_up, to_down)
    copy = pltpu.make_async_copy(frames.at[leaving], far, sem)
    copy.start()
    for j in range(BLK_IN):

        @pl.when(device > 0)
        def _():
            take(base - BLK_IN + j, from_lower)

        @pl.when(device < last)
        def _():
            take(base + BLK_IN + j, from_upper)

    qkv = wq[...].astype(F32)
    parts = [qkv[:, 0, :], qkv[:, 1, :], qkv[:, 2, :], wo[...].astype(F32)]
    tiles = []
    for part in parts:
        tiles += [part[:, :128], part[:, 128:256]]
    tails = [part[:, 256:320] for part in parts]
    tiles.append(jnp.concatenate(tails[:2], axis=1))
    tiles.append(jnp.concatenate(tails[2:], axis=1))
    proj = wp[...].astype(F32)
    tiles += [proj[:, i * 128 : (i + 1) * 128] for i in range(PROJ // 128)]
    for i, tile in enumerate(tiles):
        stage[i * K_DEV : (i + 1) * K_DEV, :] = tile
    used = TILES * K_DEV
    stage[used:, :] = jnp.zeros((PACKED - used, 128), F32)
    packed[...] = stage[...].astype(BF16)
    copy.wait()


def plan_call(block_utt, block_dest, frames, w_qkv, w_out, w_proj):
    return pl.pallas_call(
        plan_kernel,
        out_shape=(
            jax.ShapeDtypeStruct((2 * CAP + 1,), jnp.int32),
            jax.ShapeDtypeStruct((PACKED, 128), BF16),
            jax.ShapeDtypeStruct((FRAMES, D), BF16),
        ),
        in_specs=[SMEM(), SMEM(), ANY(), VMEM(), VMEM(), VMEM()],
        out_specs=(SMEM(), VMEM(), VMEM()),
        scratch_shapes=[pltpu.VMEM((PACKED, 128), F32), pltpu.SemaphoreType.DMA],
        compiler_params=pltpu.CompilerParams(vmem_limit_bytes=WIDE),
        name="plan",
    )(block_utt, block_dest, frames, w_qkv.transpose(1, 0, 2), w_out.T, w_proj)


def unpack_kernel(gathered, main, proj, flat, stage):
    nz = gathered.shape[0] // PACKED
    for z in range(nz):
        flat[...] = gathered[z * PACKED : (z + 1) * PACKED, :].astype(F32)
        for i in range(TILES):
            stage[z * K_DEV : (z + 1) * K_DEV, i * 128 : (i + 1) * 128] = flat[
                i * K_DEV : (i + 1) * K_DEV, :
            ]
    main[...] = stage[:, :D].astype(BF16)
    proj[...] = stage[:, D:].astype(BF16)


def unpack_call(gathered):
    rows = gathered.shape[0] // PACKED * K_DEV
    return pl.pallas_call(
        unpack_kernel,
        out_shape=(
            jax.ShapeDtypeStruct((rows, D), BF16),
            jax.ShapeDtypeStruct((rows, PROJ), BF16),
        ),
        in_specs=[VMEM()],
        out_specs=(VMEM(), VMEM()),
        scratch_shapes=[
            pltpu.VMEM((PACKED, 128), F32),
            pltpu.VMEM((rows, D + PROJ), F32),
        ],
        compiler_params=pltpu.CompilerParams(vmem_limit_bytes=WIDE),
        cost_estimate=pl.CostEstimate(flops=0, bytes_accessed=2 * MIB, transcendentals=0),
        name="unpack",
    )(gathered)


def leave_kernel(plan, frames, near, sem):
    copy = pltpu.make_async_copy(frames.at[plan[2 * CAP]], near, sem)
    copy.start()
    copy.wait()


def leave_call(plan, frames):
    return pl.pallas_call(
        leave_kernel,
        out_shape=jax.ShapeDtypeStruct((FRAMES, D), BF16),
        in_specs=[SMEM(), ANY()],
        out_specs=VMEM(),
        scratch_shapes=[pltpu.SemaphoreType.DMA],
        compiler_params=pltpu.CompilerParams(vmem_limit_bytes=WIDE),
        cost_estimate=pl.CostEstimate(flops=0, bytes_accessed=2 * MIB, transcendentals=0),
        name="leave",
    )(plan, frames)


def layer_norm(values, gain, shift):
    centre = jnp.mean(values, axis=-1, keepdims=True)
    centred = values - centre
    spread = jnp.mean(centred * centred, axis=-1, keepdims=True)
    return centred * lax.rsqrt(spread + EPS) * gain + shift


def split_exact(values):
    high = values.astype(BF16)
    rest = values - high.astype(F32)
    middle = rest.astype(BF16)
    low = (rest - middle.astype(F32)).astype(BF16)
    return [high, middle, low]


def prepare_kernel(
    plan, frames, far, near, gain, shift, post_gain, post_shift, order,
    normed, residual, post, blocks, stack, sems,
):
    for g in range(CAP):
        source = plan[g]

        @pl.when((source >= 0) & (source < BLK_IN))
        def _():
            pltpu.make_async_copy(frames.at[source], blocks.at[g], sems.at[g]).start()

        @pl.when(source == BLK_IN)
        def _():
            pltpu.make_async_copy(far, blocks.at[g], sems.at[g]).start()

        @pl.when(source == BLK_IN + 1)
        def _():
            pltpu.make_async_copy(near, blocks.at[g], sems.at[g]).start()

        @pl.when(source < 0)
        def _():
            blocks[g] = jnp.zeros((FRAMES, D), BF16)

    row = (1, D)
    gain, shift = gain[...].reshape(row), shift[...].reshape(row)
    parts = split_exact(post_gain[...].reshape(row))
    parts += split_exact(post_shift[...].reshape(row))
    stack[ROWS + FRAMES :, :] = jnp.concatenate(
        parts + [jnp.zeros((10, D), BF16)], axis=0
    )
    for g in range(CAP):

        @pl.when(plan[g] >= 0)
        def _():
            pltpu.make_async_copy(far, blocks.at[g], sems.at[g]).wait()

    rows = lax.broadcasted_iota(jnp.int32, (FRAMES, FRAMES), 0)
    cols = lax.broadcasted_iota(jnp.int32, (FRAMES, FRAMES), 1)
    picked = jnp.where(rows < HALF, 2 * rows, 2 * (rows - HALF) + 1)
    parity = jnp.where(cols == picked, 1.0, 0.0).astype(BF16)
    for g in range(CAP):
        sorted_rows = jnp.dot(parity, blocks[g], preferred_element_type=F32)
        done = layer_norm(sorted_rows, gain, shift).astype(BF16)
        stack[g * HALF : (g + 1) * HALF, :] = done[:HALF]
        stack[POOLED + g * HALF : POOLED + (g + 1) * HALF, :] = done[HALF:]
    own = blocks[lax.axis_index("section")]
    stack[ROWS : ROWS + FRAMES, :] = jnp.dot(
        parity, own, preferred_element_type=F32
    ).astype(BF16)
    for start in range(0, D, 256):
        feature = lax.broadcasted_iota(jnp.int32, (D, 256), 0)
        wanted = order[:, start : start + 256]
        select = jnp.where(feature == wanted, 1.0, 0.0).astype(BF16)
        moved = jnp.dot(stack[...], select, preferred_element_type=F32)
        span = slice(start, start + 256)
        normed[:, span] = moved[:ROWS].astype(BF16)
        residual[:, span] = 0.5 * (
            moved[ROWS : ROWS + HALF] + moved[ROWS + HALF : ROWS + FRAMES]
        )
        tail = moved[ROWS + FRAMES :]
        post[0:1, span] = tail[0:1] + (tail[1:2] + tail[2:3])
        post[1:2, span] = tail[3:4] + (tail[4:5] + tail[5:6])


def prepare_call(plan, frames, far, near, vectors, order):
    return pl.pallas_call(
        prepare_kernel,
        out_shape=(
            jax.ShapeDtypeStruct((ROWS, D), BF16),
            jax.ShapeDtypeStruct((HALF, D), F32),
            jax.ShapeDtypeStruct((2, D), F32),
        ),
        in_specs=[SMEM(), ANY(), ANY(), ANY()] + [VMEM()] * 5,
        out_specs=(VMEM(), VMEM(), VMEM()),
        scratch_shapes=[
            pltpu.VMEM((CAP, FRAMES, D), BF16),
            pltpu.VMEM((ROWS + FRAMES + 16, D), BF16),
            pltpu.SemaphoreType.DMA((CAP,)),
        ],
        compiler_params=pltpu.CompilerParams(vmem_limit_bytes=WIDE),
        cost_estimate=pl.CostEstimate(
            flops=8 * 656 * D * D, bytes_accessed=8 * MIB, transcendentals=0
        ),
        name="prepare",
    )(plan, frames, far, near, *vectors, order)


def main_order(y, core):
    return [(y + r) % NY for r in Y_ORDER]


def proj_order(y, core):
    first = jnp.where(core == 0, y ^ 1, y ^ 3)
    second = jnp.where(core == 0, y ^ 3, y ^ 1)
    return [y, first, second, y ^ 2]


def slab_copies(order, mine, other, weights, sems):
    core = lax.axis_index("core")
    y = lax.axis_index("y")
    copies = []
    for i, (source, side) in enumerate(((mine, core), (other, 1 - core))):
        for j, place in enumerate(order(y, side)):
            row = pl.multiple_of((place * NC + side) * SLAB, 32)
            copies.append(
                pltpu.make_async_copy(
                    source.at[pl.ds(j * SLAB, SLAB)],
                    weights.at[pl.ds(row, SLAB)],
                    sems.at[i * NY + j],
                )
            )
    return copies


def attend_kernel(plan, normed, mine, other, terms, weights, sems):
    copies = slab_copies(main_order, mine, other, weights, sems)
    for copy in copies:
        copy.start()
    slot_row = lax.broadcasted_iota(jnp.int32, (ROWS, 1), 0) % POOLED // HALF
    slot_col = lax.broadcasted_iota(jnp.int32, (1, ROWS), 1) % POOLED // HALF
    owner_row = jnp.full((ROWS, 1), -1, jnp.int32)
    owner_col = jnp.full((1, ROWS), -1, jnp.int32)
    for g in range(CAP):
        owner = plan[CAP + g]
        owner_row = jnp.where(slot_row == g, owner, owner_row)
        owner_col = jnp.where(slot_col == g, owner, owner_col)
    same = owner_row == owner_col
    low = lax.broadcasted_iota(jnp.int32, (1, 128), 1) < HEAD
    for copy in copies:
        copy.wait()
    x = normed[...]

    def project(start, size):
        return jnp.dot(x, weights[:, start : start + size], preferred_element_type=F32)

    def head(query, keyed, valued, use_low):
        query = jnp.where(low == use_low, query, 0.0).astype(BF16)
        scores = lax.dot_general(query, keyed, NT, preferred_element_type=F32)
        scores = jnp.where(same, scores * HEAD ** (-0.5), NEG)
        peak = jnp.max(scores, axis=1, keepdims=True)
        weight = jnp.exp(scores - peak)
        total = jnp.sum(weight, axis=1, keepdims=True)
        weight = (weight / total).astype(BF16)
        out = jnp.dot(weight, valued, preferred_element_type=F32)
        return 0.5 * (out[:POOLED] + out[POOLED:])

    queries = project(0, 256)
    keys = project(256, 256).astype(BF16)
    values = project(512, 256).astype(BF16)
    tail = project(1024, 256)
    pieces = []
    for pair in range(2):
        span = slice(pair * 128, (pair + 1) * 128)
        query, keyed, valued = queries[:, span], keys[:, span], values[:, span]
        first = head(query, keyed, valued, True)
        second = head(query, keyed, valued, False)
        pieces.append(jnp.where(low, first, second).astype(BF16))
    pair = tail[:, :128]
    rolled = pltpu.roll(pair, HEAD, 1).astype(BF16)
    fifth = head(pair, rolled, tail[:, 128:].astype(BF16), True)
    fifth = pltpu.roll(fifth, HEAD, 1)
    fifth = jnp.where(low, 0.0, fifth).astype(BF16)
    pooled = jnp.concatenate(pieces + [fifth], axis=1)
    for start in range(0, D, 256):
        rows = slice(start, start + 256)
        out = lax.dot_general(
            pooled[:, :256], weights[rows, 768:1024], NT, preferred_element_type=F32
        ) + lax.dot_general(
            pooled[:, 256:], weights[rows, 1152:1280], NT, preferred_element_type=F32
        )
        terms[:, rows] = out.astype(BF16)


def attend_call(plan, normed, mine, other):
    return pl.pallas_call(
        attend_kernel,
        out_shape=jax.ShapeDtypeStruct((POOLED, D), BF16),
        in_specs=[SMEM(), VMEM(), ANY(), ANY()],
        out_specs=VMEM(),
        scratch_shapes=[
            pltpu.VMEM((D, D), BF16),
            pltpu.SemaphoreType.DMA((2 * NY,)),
        ],
        compiler_params=pltpu.CompilerParams(vmem_limit_bytes=48 * MIB),
        cost_estimate=pl.CostEstimate(
            flops=3 * 10**9, bytes_accessed=8 * MIB, transcendentals=5 * ROWS * ROWS
        ),
        name="attend",
    )(plan, normed, mine, other)


def finish_kernel(terms, residual, post, out):
    total = residual[...]
    for s in range(terms.shape[0] // HALF):
        total += terms[s * HALF : (s + 1) * HALF, :].astype(F32)
    out[...] = layer_norm(total, post[0:1, :], post[1:2, :]).astype(BF16)


def finish_call(terms, residual, post):
    return pl.pallas_call(
        finish_kernel,
        out_shape=jax.ShapeDtypeStruct((HALF, D), BF16),
        in_specs=[VMEM()] * 3,
        out_specs=VMEM(),
        compiler_params=pltpu.CompilerParams(vmem_limit_bytes=16 * MIB),
        name="finish",
    )(terms, residual, post)


def project_kernel(plan, rows, mine, other, bias, out, weights, sems):
    copies = slab_copies(proj_order, mine, other, weights, sems)
    for copy in copies:
        copy.start()
    for copy in copies:
        copy.wait()
    for g in range(CAP):
        span = slice(g * HALF, (g + 1) * HALF)
        value = jnp.dot(rows[span, :], weights[...], preferred_element_type=F32)
        value = value + bias[...]
        out[span, :] = jnp.where(plan[CAP + g] >= 0, value, 0.0).astype(BF16)


def project_call(plan, rows, mine, other, bias):
    return pl.pallas_call(
        project_kernel,
        out_shape=jax.ShapeDtypeStruct((POOLED, PROJ), BF16),
        in_specs=[SMEM(), VMEM(), ANY(), ANY(), VMEM()],
        out_specs=VMEM(),
        scratch_shapes=[
            pltpu.VMEM((D, PROJ), BF16),
            pltpu.SemaphoreType.DMA((2 * NY,)),
        ],
        compiler_params=pltpu.CompilerParams(vmem_limit_bytes=48 * MIB),
        cost_estimate=pl.CostEstimate(
            flops=2 * POOLED * D * PROJ, bytes_accessed=4 * MIB, transcendentals=0
        ),
        name="project",
    )(plan, rows, mine, other, bias)


def y_slabs(slab):
    slabs = [slab]
    for r in Y_ORDER[1:]:
        slabs.append(lax.ppermute(slab, "y", [((i + r) % NY, i) for i in range(NY)]))
    return jnp.concatenate(slabs, axis=0)


def y_swap(slabs, masks):
    pairs = [
        (y * NC + core, (y ^ masks[core]) * NC + core)
        for y in range(NY)
        for core in range(NC)
    ]
    return lax.ppermute(slabs, ("y", "core"), pairs)


def other_core(slabs):
    return lax.ppermute(slabs, "core", [(0, 1), (1, 0)])


def shards(
    frames,
    block_utt,
    block_dest,
    ln_gain,
    ln_shift,
    w_qkv,
    w_out,
    post_gain,
    post_shift,
    w_proj,
    proj_bias,
):
    plan, packed, far = plan_call(
        block_utt, block_dest, frames, w_qkv, w_out, w_proj
    )
    odd = range(1, lax.axis_size(DP) - 1, 2)
    far = lax.ppermute(
        far, DP, [(i, i + 1) for i in odd] + [(i + 1, i) for i in odd]
    )
    gathered = lax.all_gather(packed, "z", axis=0, tiled=True)
    main, proj = unpack_call(gathered)
    main, plan = lax.optimization_barrier((main, plan))
    mine = y_slabs(main)
    near = other_core(leave_call(plan, frames))
    order = feature_order(lax.axis_size("z"))
    vectors = (ln_gain, ln_shift, post_gain, post_shift)
    normed, residual, post = prepare_call(plan, frames, far, near, vectors, order)
    mine, normed, proj = lax.optimization_barrier((mine, normed, proj))
    other = other_core(mine)
    proj_pair = y_swap(proj, (1, 3))
    terms = attend_call(plan, normed, mine, other)
    terms, proj_pair = lax.optimization_barrier((terms, proj_pair))
    proj_pair = jnp.concatenate([proj, proj_pair], axis=0)
    proj_rest = y_swap(proj_pair, (3, 1))
    terms = lax.all_to_all(terms, "section", split_axis=0, concat_axis=0, tiled=True)
    pooled_norm = finish_call(terms, residual, post)
    pooled_norm, proj_rest = lax.optimization_barrier((pooled_norm, proj_rest))
    proj_mine = jnp.concatenate([proj_pair, proj_rest], axis=0)
    proj_other = other_core(proj_mine)
    rows = lax.all_gather(pooled_norm, "section", axis=0, tiled=True)
    bias = proj_bias.reshape(1, PROJ)
    lm_local = project_call(plan, rows, proj_mine, proj_other, bias)
    return lax.all_to_all(lm_local, "section", split_axis=0, concat_axis=1, tiled=True)


def solution(mesh):
    dp, section = mesh.devices.shape
    shape = (dp // (NY * NC), NY, NC, section)
    fine = Mesh(mesh.devices.reshape(shape), DP + ("section",))
    return jax.shard_map(
        shards,
        mesh=fine,
        in_specs=(
            P(DP, None, None),
            P(),
            P(),
            P(),
            P(),
            P(None, DP, "section"),
            P("section", DP),
            P(),
            P(),
            P(DP, "section"),
            P("section"),
        ),
        out_specs=P(DP + ("section",), None),
        check_vma=False,
    )
```

```python
import functools

import jax
import jax.numpy as jnp
from jax import lax
from jax.experimental import pallas as pl
from jax.experimental.pallas import tpu as pltpu
from jax.sharding import Mesh, PartitionSpec as P

CAP = 4
BLK_IN = 6
FRAMES = 128
D = 1280
HEAD = 64
PART = 320
PROJ = 1024
NY = 4
NC = 2
Y_ORDER = (0, 2, 1, 3)
K_DEV = 10
TILES = 18
PACKED = 192
SLAB = 160
HALF_D = 640
HALF = FRAMES // 2
POOLED = CAP * HALF
ROWS = CAP * FRAMES
EPS = 1e-05
NEG = -1e30
F32 = jnp.float32
BF16 = jnp.bfloat16
DP = ("z", "y", "core")
MIB = 1024 * 1024
WIDE = 58 * MIB

VMEM = functools.partial(pl.BlockSpec, memory_space=pltpu.VMEM)
SMEM = functools.partial(pl.BlockSpec, memory_space=pltpu.SMEM)
ANY = functools.partial(pl.BlockSpec, memory_space=pl.ANY)

NT = (((1,), (1,)), ((), ()))


def dp_index():
    return (lax.axis_index("z") * NY + lax.axis_index("y")) * NC + lax.axis_index("core")


def y_step(index):
    return jnp.where(index == 1, 2, jnp.where(index == 2, 1, index))


def feature_at(position):
    side, rest = position // HALF_D, position % HALF_D
    place = (lax.axis_index("y") + y_step(rest // SLAB)) % NY
    core = (lax.axis_index("core") + side) % NC
    rest = rest % SLAB
    owner = (rest // K_DEV * NY + place) * NC + core
    return owner * K_DEV + rest % K_DEV


def plan_kernel(utt, dest, frames, wq, wo, wp, plan, packed, far, near, stage, sems):
    core = lax.axis_index("core")
    device = dp_index()
    last = dest.shape[0] // BLK_IN - 1
    base = device * BLK_IN
    to_down = jnp.int32(0)
    to_up = jnp.int32(0)
    from_lower = BLK_IN + core
    from_upper = BLK_IN + 1 - core
    for g in range(2 * CAP):
        plan[g] = -1

    def take(position, code):
        target = dest[position]

        @pl.when((target >= 0) & (target // CAP == device))
        def _():
            slot = target % CAP
            plan[slot] = code
            plan[CAP + slot] = utt[position]

        return target

    for j in range(BLK_IN):
        target = take(base + j, j)
        owner = jnp.where(target >= 0, target // CAP, -9)
        to_down = jnp.where(owner == device - 1, j, to_down)
        to_up = jnp.where(owner == device + 1, j, to_up)
    to_far = jnp.where(core == 0, to_down, to_up)
    to_near = jnp.where(core == 0, to_up, to_down)
    copies = [
        pltpu.make_async_copy(frames.at[to_far], far, sems.at[0]),
        pltpu.make_async_copy(frames.at[to_near], near, sems.at[1]),
    ]
    for copy in copies:
        copy.start()
    for j in range(BLK_IN):

        @pl.when(device > 0)
        def _():
            take(base - BLK_IN + j, from_lower)

        @pl.when(device < last)
        def _():
            take(base + BLK_IN + j, from_upper)

    qkv = wq[...].astype(F32)
    parts = [qkv[:, 0, :], qkv[:, 1, :], qkv[:, 2, :], wo[...].astype(F32)]
    tiles = []
    for part in parts:
        tiles += [part[:, :128], part[:, 128:256]]
    tails = [part[:, 256:320] for part in parts]
    tiles.append(jnp.concatenate(tails[:2], axis=1))
    tiles.append(jnp.concatenate(tails[2:], axis=1))
    proj = wp[...].astype(F32)
    tiles += [proj[:, i * 128 : (i + 1) * 128] for i in range(PROJ // 128)]
    for i, tile in enumerate(tiles):
        stage[i * K_DEV : (i + 1) * K_DEV, :] = tile
    used = TILES * K_DEV
    stage[used:, :] = jnp.zeros((PACKED - used, 128), F32)
    packed[...] = stage[...].astype(BF16)
    for copy in copies:
        copy.wait()


def plan_call(block_utt, block_dest, frames, w_qkv, w_out, w_proj):
    return pl.pallas_call(
        plan_kernel,
        out_shape=(
            jax.ShapeDtypeStruct((2 * CAP,), jnp.int32),
            jax.ShapeDtypeStruct((PACKED, 128), BF16),
            jax.ShapeDtypeStruct((FRAMES, D), BF16),
            jax.ShapeDtypeStruct((FRAMES, D), BF16),
        ),
        in_specs=[SMEM(), SMEM(), ANY(), VMEM(), VMEM(), VMEM()],
        out_specs=(SMEM(), VMEM(), VMEM(), VMEM()),
        scratch_shapes=[pltpu.VMEM((PACKED, 128), F32), pltpu.SemaphoreType.DMA((2,))],
        compiler_params=pltpu.CompilerParams(vmem_limit_bytes=WIDE),
        name="plan",
    )(block_utt, block_dest, frames, w_qkv.transpose(1, 0, 2), w_out.T, w_proj)


def unpack_kernel(gathered, main, proj, flat, stage):
    nz = gathered.shape[0] // PACKED
    for z in range(nz):
        flat[...] = gathered[z * PACKED : (z + 1) * PACKED, :].astype(F32)
        for i in range(TILES):
            stage[z * K_DEV : (z + 1) * K_DEV, i * 128 : (i + 1) * 128] = flat[
                i * K_DEV : (i + 1) * K_DEV, :
            ]
    main[...] = stage[:, :D].astype(BF16)
    proj[...] = stage[:, D:].astype(BF16)


def unpack_call(gathered):
    rows = gathered.shape[0] // PACKED * K_DEV
    return pl.pallas_call(
        unpack_kernel,
        out_shape=(
            jax.ShapeDtypeStruct((rows, D), BF16),
            jax.ShapeDtypeStruct((rows, PROJ), BF16),
        ),
        in_specs=[VMEM()],
        out_specs=(VMEM(), VMEM()),
        scratch_shapes=[
            pltpu.VMEM((PACKED, 128), F32),
            pltpu.VMEM((rows, D + PROJ), F32),
        ],
        compiler_params=pltpu.CompilerParams(vmem_limit_bytes=32 * MIB),
        cost_estimate=pl.CostEstimate(flops=0, bytes_accessed=2 * MIB, transcendentals=0),
        name="unpack",
    )(gathered)


def layer_norm(values, gain, shift):
    centre = jnp.mean(values, axis=-1, keepdims=True)
    centred = values - centre
    spread = jnp.mean(centred * centred, axis=-1, keepdims=True)
    return centred * lax.rsqrt(spread + EPS) * gain + shift


def split_exact(values):
    high = values.astype(BF16)
    rest = values - high.astype(F32)
    middle = rest.astype(BF16)
    low = (rest - middle.astype(F32)).astype(BF16)
    return [high, middle, low]


def parity_rows():
    rows = lax.broadcasted_iota(jnp.int32, (FRAMES, FRAMES), 0)
    cols = lax.broadcasted_iota(jnp.int32, (FRAMES, FRAMES), 1)
    picked = jnp.where(rows < HALF, 2 * rows, 2 * (rows - HALF) + 1)
    return jnp.where(cols == picked, 1.0, 0.0).astype(BF16)


def feature_select(start):
    feature = lax.broadcasted_iota(jnp.int32, (D, 256), 0)
    position = lax.broadcasted_iota(jnp.int32, (1, 256), 1) + start
    return jnp.where(feature == feature_at(position), 1.0, 0.0).astype(BF16)


def prepare_kernel(
    plan, frames, near, gain, shift, post_gain, post_shift,
    normed, residual, post, blocks, stack, sems,
):
    for g in range(CAP):
        source = plan[g]

        @pl.when((source >= 0) & (source < BLK_IN))
        def _():
            pltpu.make_async_copy(frames.at[source], blocks.at[g], sems.at[g]).start()

        @pl.when(source == BLK_IN + 1)
        def _():
            pltpu.make_async_copy(near, blocks.at[g], sems.at[g]).start()

        @pl.when((source < 0) | (source == BLK_IN))
        def _():
            blocks[g] = jnp.zeros((FRAMES, D), BF16)

    row = (1, D)
    gain, shift = gain[...].reshape(row), shift[...].reshape(row)
    parts = split_exact(post_gain[...].reshape(row))
    parts += split_exact(post_shift[...].reshape(row))
    stack[ROWS + FRAMES :, :] = jnp.concatenate(
        parts + [jnp.zeros((10, D), BF16)], axis=0
    )
    for g in range(CAP):

        @pl.when((plan[g] >= 0) & (plan[g] != BLK_IN))
        def _():
            pltpu.make_async_copy(near, blocks.at[g], sems.at[g]).wait()

    parity = parity_rows()
    for g in range(CAP):
        sorted_rows = jnp.dot(parity, blocks[g], preferred_element_type=F32)
        done = layer_norm(sorted_rows, gain, shift).astype(BF16)
        stack[g * HALF : (g + 1) * HALF, :] = done[:HALF]
        stack[POOLED + g * HALF : POOLED + (g + 1) * HALF, :] = done[HALF:]
    own = blocks[lax.axis_index("section")]
    stack[ROWS : ROWS + FRAMES, :] = jnp.dot(
        parity, own, preferred_element_type=F32
    ).astype(BF16)
    for start in range(0, D, 256):
        select = feature_select(start)
        moved = jnp.dot(stack[...], select, preferred_element_type=F32)
        span = slice(start, start + 256)
        normed[:, span] = moved[:ROWS].astype(BF16)
        residual[:, span] = 0.5 * (
            moved[ROWS : ROWS + HALF] + moved[ROWS + HALF : ROWS + FRAMES]
        )
        tail = moved[ROWS + FRAMES :]
        post[0:1, span] = tail[0:1] + (tail[1:2] + tail[2:3])
        post[1:2, span] = tail[3:4] + (tail[4:5] + tail[5:6])


def prepare_call(plan, frames, near, vectors):
    return pl.pallas_call(
        prepare_kernel,
        out_shape=(
            jax.ShapeDtypeStruct((ROWS, D), BF16),
            jax.ShapeDtypeStruct((HALF, D), F32),
            jax.ShapeDtypeStruct((2, D), F32),
        ),
        in_specs=[SMEM(), ANY(), ANY()] + [VMEM()] * 4,
        out_specs=(VMEM(), VMEM(), VMEM()),
        scratch_shapes=[
            pltpu.VMEM((CAP, FRAMES, D), BF16),
            pltpu.VMEM((ROWS + FRAMES + 16, D), BF16),
            pltpu.SemaphoreType.DMA((CAP,)),
        ],
        compiler_params=pltpu.CompilerParams(vmem_limit_bytes=24 * MIB),
        cost_estimate=pl.CostEstimate(
            flops=10**8, bytes_accessed=MIB, transcendentals=0
        ),
        name="prepare",
    )(plan, frames, near, *vectors)


def add_far_kernel(
    plan, far, gain, shift, normed_in, residual_in, normed, residual,
    stack, moved, pooled, sems,
):
    slot = jnp.int32(-1)
    for g in range(CAP):
        slot = jnp.where(plan[g] == BLK_IN, g, slot)
    own = slot == lax.axis_index("section")

    @pl.when(slot >= 0)
    def _():
        row = (1, D)
        placed = jnp.dot(parity_rows(), far[...], preferred_element_type=F32)
        done = layer_norm(placed, gain[...].reshape(row), shift[...].reshape(row))
        stack[:FRAMES, :] = done.astype(BF16)
        stack[FRAMES:, :] = placed.astype(BF16)
        for start in range(0, D, 256):
            span = slice(start, start + 256)
            out = jnp.dot(stack[...], feature_select(start), preferred_element_type=F32)
            moved[:, span] = out[:FRAMES].astype(BF16)
            pooled[:, span] = 0.5 * (out[FRAMES : FRAMES + HALF] + out[FRAMES + HALF :])
        copies = [
            pltpu.make_async_copy(
                moved.at[pl.ds(i * HALF, HALF)],
                normed.at[pl.ds(pl.multiple_of(i * POOLED + slot * HALF, HALF), HALF)],
                sems.at[i],
            )
            for i in range(2)
        ]
        for copy in copies:
            copy.start()

        @pl.when(own)
        def _():
            copy = pltpu.make_async_copy(pooled, residual, sems.at[2])
            copy.start()
            copy.wait()

        for copy in copies:
            copy.wait()


def add_far_call(plan, far, gain, shift, normed, residual):
    return pl.pallas_call(
        add_far_kernel,
        out_shape=(
            jax.ShapeDtypeStruct((ROWS, D), BF16),
            jax.ShapeDtypeStruct((HALF, D), F32),
        ),
        in_specs=[SMEM(), VMEM(), VMEM(), VMEM(), ANY(), ANY()],
        out_specs=(ANY(), ANY()),
        scratch_shapes=[
            pltpu.VMEM((2 * FRAMES, D), BF16),
            pltpu.VMEM((FRAMES, D), BF16),
            pltpu.VMEM((HALF, D), F32),
            pltpu.SemaphoreType.DMA((3,)),
        ],
        input_output_aliases={4: 0, 5: 1},
        compiler_params=pltpu.CompilerParams(vmem_limit_bytes=24 * MIB),
        cost_estimate=pl.CostEstimate(
            flops=10**8, bytes_accessed=MIB, transcendentals=0
        ),
        name="add_far",
    )(plan, far, gain, shift, normed, residual)


def attend_kernel(plan, normed, mine, other, terms):
    slot_row = lax.broadcasted_iota(jnp.int32, (ROWS, 1), 0) % POOLED // HALF
    slot_col = lax.broadcasted_iota(jnp.int32, (1, ROWS), 1) % POOLED // HALF
    owner_row = jnp.full((ROWS, 1), -1, jnp.int32)
    owner_col = jnp.full((1, ROWS), -1, jnp.int32)
    for g in range(CAP):
        owner = plan[CAP + g]
        owner_row = jnp.where(slot_row == g, owner, owner_row)
        owner_col = jnp.where(slot_col == g, owner, owner_col)
    same = owner_row == owner_col
    low = lax.broadcasted_iota(jnp.int32, (1, 128), 1) < HEAD
    left, right = normed[:, :HALF_D], normed[:, HALF_D:]

    def project(start, size):
        span = slice(start, start + size)
        return jnp.dot(left, mine[:, span], preferred_element_type=F32) + jnp.dot(
            right, other[:, span], preferred_element_type=F32
        )

    def head(query, keyed, valued, use_low):
        query = jnp.where(low == use_low, query * HEAD ** (-0.5), 0.0).astype(BF16)
        scores = lax.dot_general(query, keyed, NT, preferred_element_type=F32)
        scores = jnp.where(same, scores, NEG)
        peak = jnp.max(scores, axis=1, keepdims=True)
        weight = jnp.exp(scores - peak)
        total = jnp.sum(weight, axis=1, keepdims=True)
        weight = (weight * (1.0 / total)).astype(BF16)
        out = jnp.dot(weight, valued, preferred_element_type=F32)
        return 0.5 * (out[:POOLED] + out[POOLED:])

    queries = project(0, 256)
    keys = project(256, 256).astype(BF16)
    values = project(512, 256).astype(BF16)
    tail = project(1024, 256)
    pieces = []
    for pair in range(2):
        span = slice(pair * 128, (pair + 1) * 128)
        query, keyed, valued = queries[:, span], keys[:, span], values[:, span]
        first = head(query, keyed, valued, True)
        second = head(query, keyed, valued, False)
        pieces.append(jnp.where(low, first, second).astype(BF16))
    pair = tail[:, :128]
    rolled = pltpu.roll(pair, HEAD, 1).astype(BF16)
    fifth = head(pair, rolled, tail[:, 128:].astype(BF16), True)
    fifth = pltpu.roll(fifth, HEAD, 1)
    fifth = jnp.where(low, 0.0, fifth).astype(BF16)
    pooled = jnp.concatenate(pieces + [fifth], axis=1)
    for side, weights in enumerate((mine, other)):
        for start in range(0, HALF_D, 128):
            rows = slice(start, start + 128)
            out = lax.dot_general(
                pooled[:, :256], weights[rows, 768:1024], NT, preferred_element_type=F32
            ) + lax.dot_general(
                pooled[:, 256:], weights[rows, 1152:1280], NT, preferred_element_type=F32
            )
            start += side * HALF_D
            terms[:, start : start + 128] = out.astype(BF16)


def attend_call(plan, normed, mine, other):
    return pl.pallas_call(
        attend_kernel,
        out_shape=jax.ShapeDtypeStruct((POOLED, D), BF16),
        in_specs=[SMEM(), VMEM(), VMEM(), VMEM()],
        out_specs=VMEM(),
        compiler_params=pltpu.CompilerParams(vmem_limit_bytes=24 * MIB),
        cost_estimate=pl.CostEstimate(
            flops=3 * 10**9, bytes_accessed=8 * MIB, transcendentals=5 * ROWS * ROWS
        ),
        name="attend",
    )(plan, normed, mine, other)


def finish_kernel(terms, residual, post, out):
    total = residual[...]
    for s in range(terms.shape[0] // HALF):
        total += terms[s * HALF : (s + 1) * HALF, :].astype(F32)
    out[...] = layer_norm(total, post[0:1, :], post[1:2, :]).astype(BF16)


def finish_call(terms, residual, post):
    return pl.pallas_call(
        finish_kernel,
        out_shape=jax.ShapeDtypeStruct((HALF, D), BF16),
        in_specs=[VMEM()] * 3,
        out_specs=VMEM(),
        compiler_params=pltpu.CompilerParams(vmem_limit_bytes=16 * MIB),
        name="finish",
    )(terms, residual, post)


def slab_copies(mine, other, weights, sems):
    core = lax.axis_index("core")
    y = lax.axis_index("y")
    copies = []
    for side, source in enumerate((mine, other)):
        swapped = (core + side) % NC
        first = jnp.where(swapped == 0, y ^ 1, y ^ 3)
        second = jnp.where(swapped == 0, y ^ 3, y ^ 1)
        for j, place in enumerate((y, first, second, y ^ 2)):
            row = side * HALF_D + y_step((place - y + NY) % NY) * SLAB
            copies.append(
                pltpu.make_async_copy(
                    source.at[pl.ds(j * SLAB, SLAB)],
                    weights.at[pl.ds(pl.multiple_of(row, 32), SLAB)],
                    sems.at[side * NY + j],
                )
            )
    return copies


def project_kernel(plan, rows, mine, other, bias, out, weights, sems):
    copies = slab_copies(mine, other, weights, sems)
    for copy in copies:
        copy.start()
    slot = lax.broadcasted_iota(jnp.int32, (POOLED, 1), 0) // HALF
    live = jnp.full((POOLED, 1), -1, jnp.int32)
    for g in range(CAP):
        live = jnp.where(slot == g, plan[CAP + g], live)
    for copy in copies:
        copy.wait()
    for start in range(0, PROJ, 256):
        span = slice(start, start + 256)
        value = jnp.dot(rows[...], weights[:, span], preferred_element_type=F32)
        value = value + bias[:, span]
        out[:, span] = jnp.where(live >= 0, value, 0.0).astype(BF16)


def project_call(plan, rows, mine, other, bias):
    return pl.pallas_call(
        project_kernel,
        out_shape=jax.ShapeDtypeStruct((POOLED, PROJ), BF16),
        in_specs=[SMEM(), VMEM(), ANY(), ANY(), VMEM()],
        out_specs=VMEM(),
        scratch_shapes=[
            pltpu.VMEM((D, PROJ), BF16),
            pltpu.SemaphoreType.DMA((2 * NY,)),
        ],
        compiler_params=pltpu.CompilerParams(vmem_limit_bytes=24 * MIB),
        cost_estimate=pl.CostEstimate(
            flops=2 * POOLED * D * PROJ, bytes_accessed=4 * MIB, transcendentals=0
        ),
        name="project",
    )(plan, rows, mine, other, bias)


def y_slabs(slab):
    slabs = [slab]
    for r in Y_ORDER[1:]:
        slabs.append(lax.ppermute(slab, "y", [((i + r) % NY, i) for i in range(NY)]))
    return jnp.concatenate(slabs, axis=0)


def y_swap(slabs, masks):
    pairs = [
        (y * NC + core, (y ^ masks[core]) * NC + core)
        for y in range(NY)
        for core in range(NC)
    ]
    return lax.ppermute(slabs, ("y", "core"), pairs)


def other_core(slabs):
    return lax.ppermute(slabs, "core", [(0, 1), (1, 0)])


def shards(
    frames,
    block_utt,
    block_dest,
    ln_gain,
    ln_shift,
    w_qkv,
    w_out,
    post_gain,
    post_shift,
    w_proj,
    proj_bias,
):
    plan, packed, far, near = plan_call(
        block_utt, block_dest, frames, w_qkv, w_out, w_proj
    )
    gathered = lax.all_gather(packed, "z", axis=0, tiled=True)
    main, proj = unpack_call(gathered)
    main, far, near = lax.optimization_barrier((main, far, near))
    mine = y_slabs(main)
    odd = range(1, lax.axis_size(DP) - 1, 2)
    far = lax.ppermute(far, DP, [(i, i + 1) for i in odd] + [(i + 1, i) for i in odd])
    near, proj = lax.optimization_barrier((other_core(near), proj))
    proj_pair = jnp.concatenate([proj, y_swap(proj, (1, 3))], axis=0)
    vectors = (ln_gain, ln_shift, post_gain, post_shift)
    normed, residual, post = prepare_call(plan, frames, near, vectors)
    normed, residual = add_far_call(plan, far, ln_gain, ln_shift, normed, residual)
    mine, normed, proj_pair = lax.optimization_barrier((mine, normed, proj_pair))
    other = other_core(mine)
    proj_rest = y_swap(proj_pair, (3, 1))
    terms = attend_call(plan, normed, mine, other)
    terms = lax.all_to_all(terms, "section", split_axis=0, concat_axis=0, tiled=True)
    pooled_norm = finish_call(terms, residual, post)
    pooled_norm, proj_rest = lax.optimization_barrier((pooled_norm, proj_rest))
    proj_mine = jnp.concatenate([proj_pair, proj_rest], axis=0)
    proj_other = other_core(proj_mine)
    rows = lax.all_gather(pooled_norm, "section", axis=0, tiled=True)
    bias = proj_bias.reshape(1, PROJ)
    lm_local = project_call(plan, rows, proj_mine, proj_other, bias)
    return lax.all_to_all(lm_local, "section", split_axis=0, concat_axis=1, tiled=True)


def solution(mesh):
    dp, section = mesh.devices.shape
    shape = (dp // (NY * NC), NY, NC, section)
    fine = Mesh(mesh.devices.reshape(shape), DP + ("section",))
    return jax.shard_map(
        shards,
        mesh=fine,
        in_specs=(
            P(DP, None, None),
            P(),
            P(),
            P(),
            P(),
            P(None, DP, "section"),
            P("section", DP),
            P(),
            P(),
            P(DP, "section"),
            P("section"),
        ),
        out_specs=P(DP + ("section",), None),
        check_vma=False,
    )
```

```python
import functools

import jax
import jax.numpy as jnp
from jax import lax
from jax.experimental import pallas as pl
from jax.experimental.pallas import tpu as pltpu
from jax.sharding import Mesh, PartitionSpec as P

CAP = 4
BLK_IN = 6
FRAMES = 128
D = 1280
HEAD = 64
PART = 320
PROJ = 1024
NY = 4
NC = 2
K_DEV = 10
TILES = 18
PACKED = 192
SLAB = 160
HALF_D = 640
HALF = FRAMES // 2
POOLED = CAP * HALF
ROWS = CAP * FRAMES
EPS = 1e-05
NEG = -1e30
F32 = jnp.float32
BF16 = jnp.bfloat16
DP = ("z", "y", "core")
MIB = 1024 * 1024
WIDE = 58 * MIB

VMEM = functools.partial(pl.BlockSpec, memory_space=pltpu.VMEM)
SMEM = functools.partial(pl.BlockSpec, memory_space=pltpu.SMEM)
ANY = functools.partial(pl.BlockSpec, memory_space=pl.ANY)

NT = (((1,), (1,)), ((), ()))


def dp_index():
    return (lax.axis_index("z") * NY + lax.axis_index("y")) * NC + lax.axis_index("core")


def feature_at(position):
    side, rest = position // HALF_D, position % HALF_D
    core = (lax.axis_index("core") + side) % NC
    steps = jnp.where(core == 0, rest // SLAB, NY - rest // SLAB)
    place = (lax.axis_index("y") + steps) % NY
    rest = rest % SLAB
    owner = (rest // K_DEV * NY + place) * NC + core
    return owner * K_DEV + rest % K_DEV


def plan_kernel(utt, dest, frames, wq, wo, wp, plan, packed, far, near, stage, sems):
    core = lax.axis_index("core")
    device = dp_index()
    last = dest.shape[0] // BLK_IN - 1
    base = device * BLK_IN
    to_down = jnp.int32(0)
    to_up = jnp.int32(0)
    from_lower = BLK_IN + core
    from_upper = BLK_IN + 1 - core
    for g in range(2 * CAP):
        plan[g] = -1

    def take(position, code):
        target = dest[position]

        @pl.when((target >= 0) & (target // CAP == device))
        def _():
            slot = target % CAP
            plan[slot] = code
            plan[CAP + slot] = utt[position]

        return target

    for j in range(BLK_IN):
        target = take(base + j, j)
        owner = jnp.where(target >= 0, target // CAP, -9)
        to_down = jnp.where(owner == device - 1, j, to_down)
        to_up = jnp.where(owner == device + 1, j, to_up)
    to_far = jnp.where(core == 0, to_down, to_up)
    to_near = jnp.where(core == 0, to_up, to_down)
    copies = [
        pltpu.make_async_copy(frames.at[to_far], far, sems.at[0]),
        pltpu.make_async_copy(frames.at[to_near], near, sems.at[1]),
    ]
    for copy in copies:
        copy.start()
    for j in range(BLK_IN):

        @pl.when(device > 0)
        def _():
            take(base - BLK_IN + j, from_lower)

        @pl.when(device < last)
        def _():
            take(base + BLK_IN + j, from_upper)

    qkv = wq[...].astype(F32)
    parts = [qkv[:, 0, :], qkv[:, 1, :], qkv[:, 2, :], wo[...].astype(F32)]
    tiles = []
    for part in parts:
        tiles += [part[:, :128], part[:, 128:256]]
    tails = [part[:, 256:320] for part in parts]
    tiles.append(jnp.concatenate(tails[:2], axis=1))
    tiles.append(jnp.concatenate(tails[2:], axis=1))
    proj = wp[...].astype(F32)
    tiles += [proj[:, i * 128 : (i + 1) * 128] for i in range(PROJ // 128)]
    for i, tile in enumerate(tiles):
        stage[i * K_DEV : (i + 1) * K_DEV, :] = tile
    used = TILES * K_DEV
    stage[used:, :] = jnp.zeros((PACKED - used, 128), F32)
    packed[...] = stage[...].astype(BF16)
    for copy in copies:
        copy.wait()


def plan_call(block_utt, block_dest, frames, w_qkv, w_out, w_proj):
    return pl.pallas_call(
        plan_kernel,
        out_shape=(
            jax.ShapeDtypeStruct((2 * CAP,), jnp.int32),
            jax.ShapeDtypeStruct((PACKED, 128), BF16),
            jax.ShapeDtypeStruct((FRAMES, D), BF16),
            jax.ShapeDtypeStruct((FRAMES, D), BF16),
        ),
        in_specs=[SMEM(), SMEM(), ANY(), VMEM(), VMEM(), VMEM()],
        out_specs=(SMEM(), VMEM(), VMEM(), VMEM()),
        scratch_shapes=[pltpu.VMEM((PACKED, 128), F32), pltpu.SemaphoreType.DMA((2,))],
        compiler_params=pltpu.CompilerParams(vmem_limit_bytes=WIDE),
        name="plan",
    )(block_utt, block_dest, frames, w_qkv.transpose(1, 0, 2), w_out.T, w_proj)


def unpack_kernel(gathered, main, proj, flat, stage):
    nz = gathered.shape[0] // PACKED
    for z in range(nz):
        flat[...] = gathered[z * PACKED : (z + 1) * PACKED, :].astype(F32)
        for i in range(TILES):
            stage[z * K_DEV : (z + 1) * K_DEV, i * 128 : (i + 1) * 128] = flat[
                i * K_DEV : (i + 1) * K_DEV, :
            ]
    main[...] = stage[:, :D].astype(BF16)
    proj[...] = stage[:, D:].astype(BF16)


def unpack_call(gathered):
    rows = gathered.shape[0] // PACKED * K_DEV
    return pl.pallas_call(
        unpack_kernel,
        out_shape=(
            jax.ShapeDtypeStruct((rows, D), BF16),
            jax.ShapeDtypeStruct((rows, PROJ), BF16),
        ),
        in_specs=[VMEM()],
        out_specs=(VMEM(), VMEM()),
        scratch_shapes=[
            pltpu.VMEM((PACKED, 128), F32),
            pltpu.VMEM((rows, D + PROJ), F32),
        ],
        compiler_params=pltpu.CompilerParams(vmem_limit_bytes=32 * MIB),
        cost_estimate=pl.CostEstimate(flops=0, bytes_accessed=2 * MIB, transcendentals=0),
        name="unpack",
    )(gathered)


def layer_norm(values, gain, shift):
    centre = jnp.mean(values, axis=-1, keepdims=True)
    centred = values - centre
    spread = jnp.mean(centred * centred, axis=-1, keepdims=True)
    return centred * lax.rsqrt(spread + EPS) * gain + shift


def split_exact(values):
    high = values.astype(BF16)
    rest = values - high.astype(F32)
    middle = rest.astype(BF16)
    low = (rest - middle.astype(F32)).astype(BF16)
    return [high, middle, low]


def parity_rows():
    rows = lax.broadcasted_iota(jnp.int32, (FRAMES, FRAMES), 0)
    cols = lax.broadcasted_iota(jnp.int32, (FRAMES, FRAMES), 1)
    picked = jnp.where(rows < HALF, 2 * rows, 2 * (rows - HALF) + 1)
    return jnp.where(cols == picked, 1.0, 0.0).astype(BF16)


def feature_select(start):
    feature = lax.broadcasted_iota(jnp.int32, (D, 256), 0)
    position = lax.broadcasted_iota(jnp.int32, (1, 256), 1) + start
    return jnp.where(feature == feature_at(position), 1.0, 0.0).astype(BF16)


def prepare_kernel(
    plan, frames, near, gain, shift, post_gain, post_shift,
    normed, residual, post, blocks, stack, sems,
):
    for g in range(CAP):
        source = plan[g]

        @pl.when((source >= 0) & (source < BLK_IN))
        def _():
            pltpu.make_async_copy(frames.at[source], blocks.at[g], sems.at[g]).start()

        @pl.when(source == BLK_IN + 1)
        def _():
            pltpu.make_async_copy(near, blocks.at[g], sems.at[g]).start()

        @pl.when((source < 0) | (source == BLK_IN))
        def _():
            blocks[g] = jnp.zeros((FRAMES, D), BF16)

    row = (1, D)
    gain, shift = gain[...].reshape(row), shift[...].reshape(row)
    parts = split_exact(post_gain[...].reshape(row))
    parts += split_exact(post_shift[...].reshape(row))
    stack[ROWS + FRAMES :, :] = jnp.concatenate(
        parts + [jnp.zeros((10, D), BF16)], axis=0
    )
    for g in range(CAP):

        @pl.when((plan[g] >= 0) & (plan[g] != BLK_IN))
        def _():
            pltpu.make_async_copy(near, blocks.at[g], sems.at[g]).wait()

    parity = parity_rows()
    for g in range(CAP):
        sorted_rows = jnp.dot(parity, blocks[g], preferred_element_type=F32)
        done = layer_norm(sorted_rows, gain, shift).astype(BF16)
        stack[g * HALF : (g + 1) * HALF, :] = done[:HALF]
        stack[POOLED + g * HALF : POOLED + (g + 1) * HALF, :] = done[HALF:]
    own = blocks[lax.axis_index("section")]
    stack[ROWS : ROWS + FRAMES, :] = jnp.dot(
        parity, own, preferred_element_type=F32
    ).astype(BF16)
    for start in range(0, D, 256):
        select = feature_select(start)
        moved = jnp.dot(stack[...], select, preferred_element_type=F32)
        span = slice(start, start + 256)
        normed[:, span] = moved[:ROWS].astype(BF16)
        residual[:, span] = 0.5 * (
            moved[ROWS : ROWS + HALF] + moved[ROWS + HALF : ROWS + FRAMES]
        )
        tail = moved[ROWS + FRAMES :]
        post[0:1, span] = tail[0:1] + (tail[1:2] + tail[2:3])
        post[1:2, span] = tail[3:4] + (tail[4:5] + tail[5:6])


def prepare_call(plan, frames, near, vectors):
    return pl.pallas_call(
        prepare_kernel,
        out_shape=(
            jax.ShapeDtypeStruct((ROWS, D), BF16),
            jax.ShapeDtypeStruct((HALF, D), F32),
            jax.ShapeDtypeStruct((2, D), F32),
        ),
        in_specs=[SMEM(), ANY(), ANY()] + [VMEM()] * 4,
        out_specs=(VMEM(), VMEM(), VMEM()),
        scratch_shapes=[
            pltpu.VMEM((CAP, FRAMES, D), BF16),
            pltpu.VMEM((ROWS + FRAMES + 16, D), BF16),
            pltpu.SemaphoreType.DMA((CAP,)),
        ],
        compiler_params=pltpu.CompilerParams(vmem_limit_bytes=24 * MIB),
        cost_estimate=pl.CostEstimate(
            flops=10**8, bytes_accessed=MIB, transcendentals=0
        ),
        name="prepare",
    )(plan, frames, near, *vectors)


def add_far_kernel(
    plan, far, gain, shift, normed_in, residual_in, normed, residual,
    stack, moved, pooled, sems,
):
    slot = jnp.int32(-1)
    for g in range(CAP):
        slot = jnp.where(plan[g] == BLK_IN, g, slot)
    own = slot == lax.axis_index("section")

    @pl.when(slot >= 0)
    def _():
        row = (1, D)
        placed = jnp.dot(parity_rows(), far[...], preferred_element_type=F32)
        done = layer_norm(placed, gain[...].reshape(row), shift[...].reshape(row))
        stack[:FRAMES, :] = done.astype(BF16)
        stack[FRAMES:, :] = placed.astype(BF16)
        for start in range(0, D, 256):
            span = slice(start, start + 256)
            out = jnp.dot(stack[...], feature_select(start), preferred_element_type=F32)
            moved[:, span] = out[:FRAMES].astype(BF16)
            pooled[:, span] = 0.5 * (out[FRAMES : FRAMES + HALF] + out[FRAMES + HALF :])
        copies = [
            pltpu.make_async_copy(
                moved.at[pl.ds(i * HALF, HALF)],
                normed.at[pl.ds(pl.multiple_of(i * POOLED + slot * HALF, HALF), HALF)],
                sems.at[i],
            )
            for i in range(2)
        ]
        for copy in copies:
            copy.start()

        @pl.when(own)
        def _():
            copy = pltpu.make_async_copy(pooled, residual, sems.at[2])
            copy.start()
            copy.wait()

        for copy in copies:
            copy.wait()


def add_far_call(plan, far, gain, shift, normed, residual):
    return pl.pallas_call(
        add_far_kernel,
        out_shape=(
            jax.ShapeDtypeStruct((ROWS, D), BF16),
            jax.ShapeDtypeStruct((HALF, D), F32),
        ),
        in_specs=[SMEM(), VMEM(), VMEM(), VMEM(), ANY(), ANY()],
        out_specs=(ANY(), ANY()),
        scratch_shapes=[
            pltpu.VMEM((2 * FRAMES, D), BF16),
            pltpu.VMEM((FRAMES, D), BF16),
            pltpu.VMEM((HALF, D), F32),
            pltpu.SemaphoreType.DMA((3,)),
        ],
        input_output_aliases={4: 0, 5: 1},
        compiler_params=pltpu.CompilerParams(vmem_limit_bytes=24 * MIB),
        cost_estimate=pl.CostEstimate(
            flops=10**8, bytes_accessed=MIB, transcendentals=0
        ),
        name="add_far",
    )(plan, far, gain, shift, normed, residual)


def attend_kernel(plan, normed, mine, other, terms):
    slot_row = lax.broadcasted_iota(jnp.int32, (ROWS, 1), 0) % POOLED // HALF
    slot_col = lax.broadcasted_iota(jnp.int32, (1, ROWS), 1) % POOLED // HALF
    owner_row = jnp.full((ROWS, 1), -1, jnp.int32)
    owner_col = jnp.full((1, ROWS), -1, jnp.int32)
    for g in range(CAP):
        owner = plan[CAP + g]
        owner_row = jnp.where(slot_row == g, owner, owner_row)
        owner_col = jnp.where(slot_col == g, owner, owner_col)
    same = owner_row == owner_col
    low = lax.broadcasted_iota(jnp.int32, (1, 128), 1) < HEAD
    left, right = normed[:, :HALF_D], normed[:, HALF_D:]

    def project(start, size):
        span = slice(start, start + size)
        return jnp.dot(left, mine[:, span], preferred_element_type=F32) + jnp.dot(
            right, other[:, span], preferred_element_type=F32
        )

    def head(query, keyed, valued, use_low):
        query = jnp.where(low == use_low, query * HEAD ** (-0.5), 0.0).astype(BF16)
        scores = lax.dot_general(query, keyed, NT, preferred_element_type=F32)
        scores = jnp.where(same, scores, NEG)
        peak = jnp.max(scores, axis=1, keepdims=True)
        weight = jnp.exp(scores - peak)
        total = jnp.sum(weight, axis=1, keepdims=True)
        weight = (weight * (1.0 / total)).astype(BF16)
        out = jnp.dot(weight, valued, preferred_element_type=F32)
        return 0.5 * (out[:POOLED] + out[POOLED:])

    queries = project(0, 256)
    keys = project(256, 256).astype(BF16)
    values = project(512, 256).astype(BF16)
    tail = project(1024, 256)
    pieces = []
    for pair in range(2):
        span = slice(pair * 128, (pair + 1) * 128)
        query, keyed, valued = queries[:, span], keys[:, span], values[:, span]
        first = head(query, keyed, valued, True)
        second = head(query, keyed, valued, False)
        pieces.append(jnp.where(low, first, second).astype(BF16))
    pair = tail[:, :128]
    rolled = pltpu.roll(pair, HEAD, 1).astype(BF16)
    fifth = head(pair, rolled, tail[:, 128:].astype(BF16), True)
    fifth = pltpu.roll(fifth, HEAD, 1)
    fifth = jnp.where(low, 0.0, fifth).astype(BF16)
    pooled = jnp.concatenate(pieces + [fifth], axis=1)
    for side, weights in enumerate((mine, other)):
        for start in range(0, HALF_D, 128):
            rows = slice(start, start + 128)
            out = lax.dot_general(
                pooled[:, :256], weights[rows, 768:1024], NT, preferred_element_type=F32
            ) + lax.dot_general(
                pooled[:, 256:], weights[rows, 1152:1280], NT, preferred_element_type=F32
            )
            start += side * HALF_D
            terms[:, start : start + 128] = out.astype(BF16)


def attend_call(plan, normed, mine, other):
    return pl.pallas_call(
        attend_kernel,
        out_shape=jax.ShapeDtypeStruct((POOLED, D), BF16),
        in_specs=[SMEM(), VMEM(), VMEM(), VMEM()],
        out_specs=VMEM(),
        compiler_params=pltpu.CompilerParams(vmem_limit_bytes=24 * MIB),
        cost_estimate=pl.CostEstimate(
            flops=3 * 10**9, bytes_accessed=8 * MIB, transcendentals=5 * ROWS * ROWS
        ),
        name="attend",
    )(plan, normed, mine, other)


def finish_kernel(terms, residual, post, out):
    total = residual[...]
    for s in range(terms.shape[0] // HALF):
        total += terms[s * HALF : (s + 1) * HALF, :].astype(F32)
    out[...] = layer_norm(total, post[0:1, :], post[1:2, :]).astype(BF16)


def finish_call(terms, residual, post):
    return pl.pallas_call(
        finish_kernel,
        out_shape=jax.ShapeDtypeStruct((HALF, D), BF16),
        in_specs=[VMEM()] * 3,
        out_specs=VMEM(),
        compiler_params=pltpu.CompilerParams(vmem_limit_bytes=16 * MIB),
        name="finish",
    )(terms, residual, post)


def project_kernel(plan, rows, mine, other, bias, out):
    slot = lax.broadcasted_iota(jnp.int32, (POOLED, 1), 0) // HALF
    live = jnp.full((POOLED, 1), -1, jnp.int32)
    for g in range(CAP):
        live = jnp.where(slot == g, plan[CAP + g], live)
    left, right = rows[:, :HALF_D], rows[:, HALF_D:]
    for start in range(0, PROJ, 256):
        span = slice(start, start + 256)
        value = jnp.dot(left, mine[:, span], preferred_element_type=F32) + jnp.dot(
            right, other[:, span], preferred_element_type=F32
        )
        value = value + bias[:, span]
        out[:, span] = jnp.where(live >= 0, value, 0.0).astype(BF16)


def project_call(plan, rows, mine, other, bias):
    return pl.pallas_call(
        project_kernel,
        out_shape=jax.ShapeDtypeStruct((POOLED, PROJ), BF16),
        in_specs=[SMEM(), VMEM(), VMEM(), VMEM(), VMEM()],
        out_specs=VMEM(),
        compiler_params=pltpu.CompilerParams(vmem_limit_bytes=24 * MIB),
        cost_estimate=pl.CostEstimate(
            flops=2 * POOLED * D * PROJ, bytes_accessed=4 * MIB, transcendentals=0
        ),
        name="project",
    )(plan, rows, mine, other, bias)


def y_shift(slabs, steps):
    pairs = [
        ((y + (NY - steps if core else steps)) % NY * NC + core, y * NC + core)
        for y in range(NY)
        for core in range(NC)
    ]
    return lax.ppermute(slabs, ("y", "core"), pairs)


def other_core(slabs):
    return lax.ppermute(slabs, "core", [(0, 1), (1, 0)])


def shards(
    frames,
    block_utt,
    block_dest,
    ln_gain,
    ln_shift,
    w_qkv,
    w_out,
    post_gain,
    post_shift,
    w_proj,
    proj_bias,
):
    plan, packed, far, near = plan_call(
        block_utt, block_dest, frames, w_qkv, w_out, w_proj
    )
    gathered = lax.all_gather(packed, "z", axis=0, tiled=True)
    main, proj = unpack_call(gathered)
    main, far, near = lax.optimization_barrier((main, far, near))
    slabs = {steps: y_shift(main, steps) for steps in (2, 1, 3)}
    mine = jnp.concatenate([main, slabs[1], slabs[2], slabs[3]], axis=0)
    odd = range(1, lax.axis_size(DP) - 1, 2)
    far = lax.ppermute(far, DP, [(i, i + 1) for i in odd] + [(i + 1, i) for i in odd])
    near, proj = lax.optimization_barrier((other_core(near), proj))
    proj_pair = jnp.concatenate([proj, y_shift(proj, 1)], axis=0)
    vectors = (ln_gain, ln_shift, post_gain, post_shift)
    normed, residual, post = prepare_call(plan, frames, near, vectors)
    normed, residual = add_far_call(plan, far, ln_gain, ln_shift, normed, residual)
    mine, normed, proj_pair = lax.optimization_barrier((mine, normed, proj_pair))
    other = other_core(mine)
    proj_rest = y_shift(proj_pair, 2)
    terms = attend_call(plan, normed, mine, other)
    terms = lax.all_to_all(terms, "section", split_axis=0, concat_axis=0, tiled=True)
    pooled_norm = finish_call(terms, residual, post)
    pooled_norm, proj_pair, proj_rest = lax.optimization_barrier(
        (pooled_norm, proj_pair, proj_rest)
    )
    proj_mine = jnp.concatenate([proj_pair, proj_rest], axis=0)
    proj_other = other_core(proj_mine)
    rows = lax.all_gather(pooled_norm, "section", axis=0, tiled=True)
    bias = proj_bias.reshape(1, PROJ)
    lm_local = project_call(plan, rows, proj_mine, proj_other, bias)
    return lax.all_to_all(lm_local, "section", split_axis=0, concat_axis=1, tiled=True)


def solution(mesh):
    dp, section = mesh.devices.shape
    shape = (dp // (NY * NC), NY, NC, section)
    fine = Mesh(mesh.devices.reshape(shape), DP + ("section",))
    return jax.shard_map(
        shards,
        mesh=fine,
        in_specs=(
            P(DP, None, None),
            P(),
            P(),
            P(),
            P(),
            P(None, DP, "section"),
            P("section", DP),
            P(),
            P(),
            P(DP, "section"),
            P("section"),
        ),
        out_specs=P(DP + ("section",), None),
        check_vma=False,
    )
```

```python
import functools

import jax
import jax.numpy as jnp
from jax import lax
from jax.experimental import pallas as pl
from jax.experimental.pallas import tpu as pltpu
from jax.sharding import Mesh, PartitionSpec as P

CAP = 4
BLK_IN = 6
FRAMES = 128
D = 1280
HEAD = 64
PART = 320
PROJ = 1024
NY = 4
NC = 2
K_DEV = 10
TILES = 18
PACKED = 192
SLAB = 160
HALF_D = 640
HALF = FRAMES // 2
POOLED = CAP * HALF
ROWS = CAP * FRAMES
EPS = 1e-05
NEG = -1e30
F32 = jnp.float32
BF16 = jnp.bfloat16
DP = ("z", "y", "core")
MIB = 1024 * 1024
WIDE = 58 * MIB

VMEM = functools.partial(pl.BlockSpec, memory_space=pltpu.VMEM)
SMEM = functools.partial(pl.BlockSpec, memory_space=pltpu.SMEM)
ANY = functools.partial(pl.BlockSpec, memory_space=pl.ANY)

NT = (((1,), (1,)), ((), ()))


def dp_index():
    return (lax.axis_index("z") * NY + lax.axis_index("y")) * NC + lax.axis_index("core")


def feature_at(position):
    side, rest = position // HALF_D, position % HALF_D
    core = (lax.axis_index("core") + side) % NC
    steps = jnp.where(core == 0, rest // SLAB, NY - rest // SLAB)
    place = (lax.axis_index("y") + steps) % NY
    rest = rest % SLAB
    owner = (rest // K_DEV * NY + place) * NC + core
    return owner * K_DEV + rest % K_DEV


def plan_kernel(utt, dest, frames, wq, wo, wp, plan, packed, far, near, stage, sems):
    core = lax.axis_index("core")
    device = dp_index()
    last = dest.shape[0] // BLK_IN - 1
    base = device * BLK_IN
    to_down = jnp.int32(0)
    to_up = jnp.int32(0)
    from_lower = BLK_IN + core
    from_upper = BLK_IN + 1 - core
    for g in range(2 * CAP):
        plan[g] = -1

    def take(position, code):
        target = dest[position]

        @pl.when((target >= 0) & (target // CAP == device))
        def _():
            slot = target % CAP
            plan[slot] = code
            plan[CAP + slot] = utt[position]

        return target

    for j in range(BLK_IN):
        target = take(base + j, j)
        owner = jnp.where(target >= 0, target // CAP, -9)
        to_down = jnp.where(owner == device - 1, j, to_down)
        to_up = jnp.where(owner == device + 1, j, to_up)
    to_far = jnp.where(core == 0, to_down, to_up)
    to_near = jnp.where(core == 0, to_up, to_down)
    copies = [
        pltpu.make_async_copy(frames.at[to_far], far, sems.at[0]),
        pltpu.make_async_copy(frames.at[to_near], near, sems.at[1]),
    ]
    for copy in copies:
        copy.start()
    for j in range(BLK_IN):

        @pl.when(device > 0)
        def _():
            take(base - BLK_IN + j, from_lower)

        @pl.when(device < last)
        def _():
            take(base + BLK_IN + j, from_upper)

    qkv = wq[...].astype(F32)
    parts = [qkv[:, 0, :], qkv[:, 1, :], qkv[:, 2, :], wo[...].astype(F32)]
    tiles = []
    for part in parts:
        tiles += [part[:, :128], part[:, 128:256]]
    tails = [part[:, 256:320] for part in parts]
    tiles.append(jnp.concatenate(tails[:2], axis=1))
    tiles.append(jnp.concatenate(tails[2:], axis=1))
    proj = wp[...].astype(F32)
    tiles += [proj[:, i * 128 : (i + 1) * 128] for i in range(PROJ // 128)]
    for i, tile in enumerate(tiles):
        stage[i * K_DEV : (i + 1) * K_DEV, :] = tile
    used = TILES * K_DEV
    stage[used:, :] = jnp.zeros((PACKED - used, 128), F32)
    packed[...] = stage[...].astype(BF16)
    for copy in copies:
        copy.wait()


def plan_call(block_utt, block_dest, frames, w_qkv, w_out, w_proj):
    return pl.pallas_call(
        plan_kernel,
        out_shape=(
            jax.ShapeDtypeStruct((2 * CAP,), jnp.int32),
            jax.ShapeDtypeStruct((PACKED, 128), BF16),
            jax.ShapeDtypeStruct((FRAMES, D), BF16),
            jax.ShapeDtypeStruct((FRAMES, D), BF16),
        ),
        in_specs=[SMEM(), SMEM(), ANY(), VMEM(), VMEM(), VMEM()],
        out_specs=(SMEM(), VMEM(), VMEM(), VMEM()),
        scratch_shapes=[pltpu.VMEM((PACKED, 128), F32), pltpu.SemaphoreType.DMA((2,))],
        compiler_params=pltpu.CompilerParams(vmem_limit_bytes=WIDE),
        name="plan",
    )(block_utt, block_dest, frames, w_qkv.transpose(1, 0, 2), w_out.T, w_proj)


def unpack_kernel(gathered, main, proj, flat, stage):
    nz = gathered.shape[0] // PACKED
    for z in range(nz):
        flat[...] = gathered[z * PACKED : (z + 1) * PACKED, :].astype(F32)
        for i in range(TILES):
            stage[z * K_DEV : (z + 1) * K_DEV, i * 128 : (i + 1) * 128] = flat[
                i * K_DEV : (i + 1) * K_DEV, :
            ]
    main[...] = stage[:, :D].astype(BF16)
    proj[...] = stage[:, D:].astype(BF16)


def unpack_call(gathered):
    rows = gathered.shape[0] // PACKED * K_DEV
    return pl.pallas_call(
        unpack_kernel,
        out_shape=(
            jax.ShapeDtypeStruct((rows, D), BF16),
            jax.ShapeDtypeStruct((rows, PROJ), BF16),
        ),
        in_specs=[VMEM()],
        out_specs=(VMEM(), VMEM()),
        scratch_shapes=[
            pltpu.VMEM((PACKED, 128), F32),
            pltpu.VMEM((rows, D + PROJ), F32),
        ],
        compiler_params=pltpu.CompilerParams(vmem_limit_bytes=32 * MIB),
        cost_estimate=pl.CostEstimate(flops=0, bytes_accessed=2 * MIB, transcendentals=0),
        name="unpack",
    )(gathered)


def layer_norm(values, gain, shift):
    centre = jnp.mean(values, axis=-1, keepdims=True)
    centred = values - centre
    spread = jnp.mean(centred * centred, axis=-1, keepdims=True)
    return centred * lax.rsqrt(spread + EPS) * gain + shift


def split_exact(values):
    high = values.astype(BF16)
    rest = values - high.astype(F32)
    middle = rest.astype(BF16)
    low = (rest - middle.astype(F32)).astype(BF16)
    return [high, middle, low]


def parity_rows():
    rows = lax.broadcasted_iota(jnp.int32, (FRAMES, FRAMES), 0)
    cols = lax.broadcasted_iota(jnp.int32, (FRAMES, FRAMES), 1)
    picked = jnp.where(rows < HALF, 2 * rows, 2 * (rows - HALF) + 1)
    return jnp.where(cols == picked, 1.0, 0.0).astype(BF16)


def feature_select(start):
    feature = lax.broadcasted_iota(jnp.int32, (D, 256), 0)
    position = lax.broadcasted_iota(jnp.int32, (1, 256), 1) + start
    return jnp.where(feature == feature_at(position), 1.0, 0.0).astype(BF16)


def prepare_kernel(
    plan, frames, near, gain, shift, post_gain, post_shift,
    normed, residual, post, blocks, stack, sems,
):
    for g in range(CAP):
        source = plan[g]

        @pl.when((source >= 0) & (source < BLK_IN))
        def _():
            pltpu.make_async_copy(frames.at[source], blocks.at[g], sems.at[g]).start()

        @pl.when(source == BLK_IN + 1)
        def _():
            pltpu.make_async_copy(near, blocks.at[g], sems.at[g]).start()

        @pl.when((source < 0) | (source == BLK_IN))
        def _():
            blocks[g] = jnp.zeros((FRAMES, D), BF16)

    row = (1, D)
    gain, shift = gain[...].reshape(row), shift[...].reshape(row)
    parts = split_exact(post_gain[...].reshape(row))
    parts += split_exact(post_shift[...].reshape(row))
    stack[ROWS + FRAMES :, :] = jnp.concatenate(
        parts + [jnp.zeros((10, D), BF16)], axis=0
    )
    for g in range(CAP):

        @pl.when((plan[g] >= 0) & (plan[g] != BLK_IN))
        def _():
            pltpu.make_async_copy(near, blocks.at[g], sems.at[g]).wait()

    parity = parity_rows()
    for g in range(CAP):
        sorted_rows = jnp.dot(parity, blocks[g], preferred_element_type=F32)
        done = layer_norm(sorted_rows, gain, shift).astype(BF16)
        stack[g * HALF : (g + 1) * HALF, :] = done[:HALF]
        stack[POOLED + g * HALF : POOLED + (g + 1) * HALF, :] = done[HALF:]
    own = blocks[lax.axis_index("section")]
    stack[ROWS : ROWS + FRAMES, :] = jnp.dot(
        parity, own, preferred_element_type=F32
    ).astype(BF16)
    for start in range(0, D, 256):
        select = feature_select(start)
        moved = jnp.dot(stack[...], select, preferred_element_type=F32)
        span = slice(start, start + 256)
        normed[:, span] = moved[:ROWS].astype(BF16)
        residual[:, span] = 0.5 * (
            moved[ROWS : ROWS + HALF] + moved[ROWS + HALF : ROWS + FRAMES]
        )
        tail = moved[ROWS + FRAMES :]
        post[0:1, span] = tail[0:1] + (tail[1:2] + tail[2:3])
        post[1:2, span] = tail[3:4] + (tail[4:5] + tail[5:6])


def prepare_call(plan, frames, near, vectors):
    return pl.pallas_call(
        prepare_kernel,
        out_shape=(
            jax.ShapeDtypeStruct((ROWS, D), BF16),
            jax.ShapeDtypeStruct((HALF, D), F32),
            jax.ShapeDtypeStruct((2, D), F32),
        ),
        in_specs=[SMEM(), ANY(), ANY()] + [VMEM()] * 4,
        out_specs=(VMEM(), VMEM(), VMEM()),
        scratch_shapes=[
            pltpu.VMEM((CAP, FRAMES, D), BF16),
            pltpu.VMEM((ROWS + FRAMES + 16, D), BF16),
            pltpu.SemaphoreType.DMA((CAP,)),
        ],
        compiler_params=pltpu.CompilerParams(vmem_limit_bytes=24 * MIB),
        cost_estimate=pl.CostEstimate(
            flops=10**8, bytes_accessed=MIB, transcendentals=0
        ),
        name="prepare",
    )(plan, frames, near, *vectors)


def add_far_kernel(
    plan, far, gain, shift, normed_in, residual_in, normed, residual,
    stack, moved, pooled, sems,
):
    slot = jnp.int32(-1)
    for g in range(CAP):
        slot = jnp.where(plan[g] == BLK_IN, g, slot)
    own = slot == lax.axis_index("section")

    @pl.when(slot >= 0)
    def _():
        row = (1, D)
        placed = jnp.dot(parity_rows(), far[...], preferred_element_type=F32)
        done = layer_norm(placed, gain[...].reshape(row), shift[...].reshape(row))
        stack[:FRAMES, :] = done.astype(BF16)
        stack[FRAMES:, :] = placed.astype(BF16)
        for start in range(0, D, 256):
            span = slice(start, start + 256)
            out = jnp.dot(stack[...], feature_select(start), preferred_element_type=F32)
            moved[:, span] = out[:FRAMES].astype(BF16)
            pooled[:, span] = 0.5 * (out[FRAMES : FRAMES + HALF] + out[FRAMES + HALF :])
        copies = [
            pltpu.make_async_copy(
                moved.at[pl.ds(i * HALF, HALF)],
                normed.at[pl.ds(pl.multiple_of(i * POOLED + slot * HALF, HALF), HALF)],
                sems.at[i],
            )
            for i in range(2)
        ]
        for copy in copies:
            copy.start()

        @pl.when(own)
        def _():
            copy = pltpu.make_async_copy(pooled, residual, sems.at[2])
            copy.start()
            copy.wait()

        for copy in copies:
            copy.wait()


def add_far_call(plan, far, gain, shift, normed, residual):
    return pl.pallas_call(
        add_far_kernel,
        out_shape=(
            jax.ShapeDtypeStruct((ROWS, D), BF16),
            jax.ShapeDtypeStruct((HALF, D), F32),
        ),
        in_specs=[SMEM(), VMEM(), VMEM(), VMEM(), ANY(), ANY()],
        out_specs=(ANY(), ANY()),
        scratch_shapes=[
            pltpu.VMEM((2 * FRAMES, D), BF16),
            pltpu.VMEM((FRAMES, D), BF16),
            pltpu.VMEM((HALF, D), F32),
            pltpu.SemaphoreType.DMA((3,)),
        ],
        input_output_aliases={4: 0, 5: 1},
        compiler_params=pltpu.CompilerParams(vmem_limit_bytes=24 * MIB),
        cost_estimate=pl.CostEstimate(
            flops=10**8, bytes_accessed=MIB, transcendentals=0
        ),
        name="add_far",
    )(plan, far, gain, shift, normed, residual)


def attend_kernel(plan, normed, mine, other, terms):
    slot_row = lax.broadcasted_iota(jnp.int32, (ROWS, 1), 0) % POOLED // HALF
    slot_col = lax.broadcasted_iota(jnp.int32, (1, ROWS), 1) % POOLED // HALF
    owner_row = jnp.full((ROWS, 1), -1, jnp.int32)
    owner_col = jnp.full((1, ROWS), -1, jnp.int32)
    for g in range(CAP):
        owner = plan[CAP + g]
        owner_row = jnp.where(slot_row == g, owner, owner_row)
        owner_col = jnp.where(slot_col == g, owner, owner_col)
    same = owner_row == owner_col
    low = lax.broadcasted_iota(jnp.int32, (1, 128), 1) < HEAD
    left, right = normed[:, :HALF_D], normed[:, HALF_D:]

    def project(start, size):
        span = slice(start, start + size)
        return jnp.dot(left, mine[:, span], preferred_element_type=F32) + jnp.dot(
            right, other[:, span], preferred_element_type=F32
        )

    def head(query, keyed, valued, use_low):
        query = jnp.where(low == use_low, query * HEAD ** (-0.5), 0.0).astype(BF16)
        scores = lax.dot_general(query, keyed, NT, preferred_element_type=F32)
        scores = jnp.where(same, scores, NEG)
        peak = jnp.max(scores, axis=1, keepdims=True)
        weight = jnp.exp(scores - peak)
        total = jnp.sum(weight, axis=1, keepdims=True)
        weight = weight * (0.5 / total)
        weight = (weight[:POOLED] + weight[POOLED:]).astype(BF16)
        return jnp.dot(weight, valued, preferred_element_type=F32)

    queries = project(0, 256)
    keys = project(256, 256).astype(BF16)
    values = project(512, 256).astype(BF16)
    tail = project(1024, 256)
    pieces = []
    for pair in range(2):
        span = slice(pair * 128, (pair + 1) * 128)
        query, keyed, valued = queries[:, span], keys[:, span], values[:, span]
        first = head(query, keyed, valued, True)
        second = head(query, keyed, valued, False)
        pieces.append(jnp.where(low, first, second).astype(BF16))
    pair = tail[:, :128]
    rolled = pltpu.roll(pair, HEAD, 1).astype(BF16)
    fifth = head(pair, rolled, tail[:, 128:].astype(BF16), True)
    fifth = pltpu.roll(fifth, HEAD, 1)
    fifth = jnp.where(low, 0.0, fifth).astype(BF16)
    pooled = jnp.concatenate(pieces + [fifth], axis=1)
    for side, weights in enumerate((mine, other)):
        for start in range(0, HALF_D, 128):
            rows = slice(start, start + 128)
            out = lax.dot_general(
                pooled[:, :256], weights[rows, 768:1024], NT, preferred_element_type=F32
            ) + lax.dot_general(
                pooled[:, 256:], weights[rows, 1152:1280], NT, preferred_element_type=F32
            )
            start += side * HALF_D
            terms[:, start : start + 128] = out.astype(BF16)


def attend_call(plan, normed, mine, other):
    return pl.pallas_call(
        attend_kernel,
        out_shape=jax.ShapeDtypeStruct((POOLED, D), BF16),
        in_specs=[SMEM(), VMEM(), VMEM(), VMEM()],
        out_specs=VMEM(),
        compiler_params=pltpu.CompilerParams(vmem_limit_bytes=24 * MIB),
        cost_estimate=pl.CostEstimate(
            flops=3 * 10**9, bytes_accessed=8 * MIB, transcendentals=5 * ROWS * ROWS
        ),
        name="attend",
    )(plan, normed, mine, other)


def finish_kernel(terms, residual, post, out):
    total = residual[...]
    for s in range(terms.shape[0] // HALF):
        total += terms[s * HALF : (s + 1) * HALF, :].astype(F32)
    out[...] = layer_norm(total, post[0:1, :], post[1:2, :]).astype(BF16)


def finish_call(terms, residual, post):
    return pl.pallas_call(
        finish_kernel,
        out_shape=jax.ShapeDtypeStruct((HALF, D), BF16),
        in_specs=[VMEM()] * 3,
        out_specs=VMEM(),
        compiler_params=pltpu.CompilerParams(vmem_limit_bytes=16 * MIB),
        name="finish",
    )(terms, residual, post)


def project_kernel(plan, rows, mine, other, bias, out):
    slot = lax.broadcasted_iota(jnp.int32, (POOLED, 1), 0) // HALF
    live = jnp.full((POOLED, 1), -1, jnp.int32)
    for g in range(CAP):
        live = jnp.where(slot == g, plan[CAP + g], live)
    left, right = rows[:, :HALF_D], rows[:, HALF_D:]
    for start in range(0, PROJ, 256):
        span = slice(start, start + 256)
        value = jnp.dot(left, mine[:, span], preferred_element_type=F32) + jnp.dot(
            right, other[:, span], preferred_element_type=F32
        )
        value = value + bias[:, span]
        out[:, span] = jnp.where(live >= 0, value, 0.0).astype(BF16)


def project_call(plan, rows, mine, other, bias):
    return pl.pallas_call(
        project_kernel,
        out_shape=jax.ShapeDtypeStruct((POOLED, PROJ), BF16),
        in_specs=[SMEM(), VMEM(), VMEM(), VMEM(), VMEM()],
        out_specs=VMEM(),
        compiler_params=pltpu.CompilerParams(vmem_limit_bytes=24 * MIB),
        cost_estimate=pl.CostEstimate(
            flops=2 * POOLED * D * PROJ, bytes_accessed=4 * MIB, transcendentals=0
        ),
        name="project",
    )(plan, rows, mine, other, bias)


def y_shift(slabs, steps):
    pairs = [
        ((y + (NY - steps if core else steps)) % NY * NC + core, y * NC + core)
        for y in range(NY)
        for core in range(NC)
    ]
    return lax.ppermute(slabs, ("y", "core"), pairs)


def other_core(slabs):
    return lax.ppermute(slabs, "core", [(0, 1), (1, 0)])


def shards(
    frames,
    block_utt,
    block_dest,
    ln_gain,
    ln_shift,
    w_qkv,
    w_out,
    post_gain,
    post_shift,
    w_proj,
    proj_bias,
):
    plan, packed, far, near = plan_call(
        block_utt, block_dest, frames, w_qkv, w_out, w_proj
    )
    gathered = lax.all_gather(packed, "z", axis=0, tiled=True)
    main, proj = unpack_call(gathered)
    main, far, near = lax.optimization_barrier((main, far, near))
    slabs = {steps: y_shift(main, steps) for steps in (2, 1, 3)}
    mine = jnp.concatenate([main, slabs[1], slabs[2], slabs[3]], axis=0)
    odd = range(1, lax.axis_size(DP) - 1, 2)
    far = lax.ppermute(far, DP, [(i, i + 1) for i in odd] + [(i + 1, i) for i in odd])
    near, proj = lax.optimization_barrier((other_core(near), proj))
    proj_pair = jnp.concatenate([proj, y_shift(proj, 1)], axis=0)
    vectors = (ln_gain, ln_shift, post_gain, post_shift)
    normed, residual, post = prepare_call(plan, frames, near, vectors)
    normed, residual = add_far_call(plan, far, ln_gain, ln_shift, normed, residual)
    mine, normed, proj_pair = lax.optimization_barrier((mine, normed, proj_pair))
    other = other_core(mine)
    proj_rest = y_shift(proj_pair, 2)
    terms = attend_call(plan, normed, mine, other)
    terms = lax.all_to_all(terms, "section", split_axis=0, concat_axis=0, tiled=True)
    pooled_norm = finish_call(terms, residual, post)
    pooled_norm, proj_pair, proj_rest = lax.optimization_barrier(
        (pooled_norm, proj_pair, proj_rest)
    )
    proj_mine = jnp.concatenate([proj_pair, proj_rest], axis=0)
    proj_other = other_core(proj_mine)
    rows = lax.all_gather(pooled_norm, "section", axis=0, tiled=True)
    bias = proj_bias.reshape(1, PROJ)
    lm_local = project_call(plan, rows, proj_mine, proj_other, bias)
    return lax.all_to_all(lm_local, "section", split_axis=0, concat_axis=1, tiled=True)


def solution(mesh):
    dp, section = mesh.devices.shape
    shape = (dp // (NY * NC), NY, NC, section)
    fine = Mesh(mesh.devices.reshape(shape), DP + ("section",))
    return jax.shard_map(
        shards,
        mesh=fine,
        in_specs=(
            P(DP, None, None),
            P(),
            P(),
            P(),
            P(),
            P(None, DP, "section"),
            P("section", DP),
            P(),
            P(),
            P(DP, "section"),
            P("section"),
        ),
        out_specs=P(DP + ("section",), None),
        check_vma=False,
    )
```

```python
import functools

import jax
import jax.numpy as jnp
from jax import lax
from jax.experimental import pallas as pl
from jax.experimental.pallas import tpu as pltpu
from jax.sharding import Mesh, PartitionSpec as P

CAP = 4
BLK_IN = 6
FRAMES = 128
D = 1280
HEAD = 64
PART = 320
PROJ = 1024
NY = 4
NC = 2
K_DEV = 10
TILES = 18
PACKED = 192
SLAB = 160
HALF_D = 640
HALF = FRAMES // 2
POOLED = CAP * HALF
ROWS = CAP * FRAMES
EPS = 1e-05
NEG = -1e30
F32 = jnp.float32
BF16 = jnp.bfloat16
DP = ("z", "y", "core")
MIB = 1024 * 1024
WIDE = 58 * MIB

VMEM = functools.partial(pl.BlockSpec, memory_space=pltpu.VMEM)
SMEM = functools.partial(pl.BlockSpec, memory_space=pltpu.SMEM)
ANY = functools.partial(pl.BlockSpec, memory_space=pl.ANY)

NT = (((1,), (1,)), ((), ()))


def dp_index():
    return (lax.axis_index("z") * NY + lax.axis_index("y")) * NC + lax.axis_index("core")


def feature_at(position):
    side, rest = position // HALF_D, position % HALF_D
    core = (lax.axis_index("core") + side) % NC
    steps = jnp.where(core == 0, rest // SLAB, NY - rest // SLAB)
    place = (lax.axis_index("y") + steps) % NY
    rest = rest % SLAB
    owner = (rest // K_DEV * NY + place) * NC + core
    return owner * K_DEV + rest % K_DEV


def plan_kernel(utt, dest, frames, wq, wo, wp, plan, packed, far, near, stage, sems):
    core = lax.axis_index("core")
    device = dp_index()
    last = dest.shape[0] // BLK_IN - 1
    base = device * BLK_IN
    to_down = jnp.int32(0)
    to_up = jnp.int32(0)
    from_lower = BLK_IN + core
    from_upper = BLK_IN + 1 - core
    for g in range(2 * CAP):
        plan[g] = -1

    def take(position, code):
        target = dest[position]

        @pl.when((target >= 0) & (target // CAP == device))
        def _():
            slot = target % CAP
            plan[slot] = code
            plan[CAP + slot] = utt[position]

        return target

    for j in range(BLK_IN):
        target = take(base + j, j)
        owner = jnp.where(target >= 0, target // CAP, -9)
        to_down = jnp.where(owner == device - 1, j, to_down)
        to_up = jnp.where(owner == device + 1, j, to_up)
    to_far = jnp.where(core == 0, to_down, to_up)
    to_near = jnp.where(core == 0, to_up, to_down)
    copies = [
        pltpu.make_async_copy(frames.at[to_far], far, sems.at[0]),
        pltpu.make_async_copy(frames.at[to_near], near, sems.at[1]),
    ]
    for copy in copies:
        copy.start()
    for j in range(BLK_IN):

        @pl.when(device > 0)
        def _():
            take(base - BLK_IN + j, from_lower)

        @pl.when(device < last)
        def _():
            take(base + BLK_IN + j, from_upper)

    qkv = wq[...].astype(F32)
    parts = [qkv[:, 0, :], qkv[:, 1, :], qkv[:, 2, :], wo[...].astype(F32)]
    tiles = []
    for part in parts:
        tiles += [part[:, :128], part[:, 128:256]]
    tails = [part[:, 256:320] for part in parts]
    tiles.append(jnp.concatenate(tails[:2], axis=1))
    tiles.append(jnp.concatenate(tails[2:], axis=1))
    proj = wp[...].astype(F32)
    tiles += [proj[:, i * 128 : (i + 1) * 128] for i in range(PROJ // 128)]
    for i, tile in enumerate(tiles):
        stage[i * K_DEV : (i + 1) * K_DEV, :] = tile
    used = TILES * K_DEV
    stage[used:, :] = jnp.zeros((PACKED - used, 128), F32)
    packed[...] = stage[...].astype(BF16)
    for copy in copies:
        copy.wait()


def plan_call(block_utt, block_dest, frames, w_qkv, w_out, w_proj):
    return pl.pallas_call(
        plan_kernel,
        out_shape=(
            jax.ShapeDtypeStruct((2 * CAP,), jnp.int32),
            jax.ShapeDtypeStruct((PACKED, 128), BF16),
            jax.ShapeDtypeStruct((FRAMES, D), BF16),
            jax.ShapeDtypeStruct((FRAMES, D), BF16),
        ),
        in_specs=[SMEM(), SMEM(), ANY(), VMEM(), VMEM(), VMEM()],
        out_specs=(SMEM(), VMEM(), VMEM(), VMEM()),
        scratch_shapes=[pltpu.VMEM((PACKED, 128), F32), pltpu.SemaphoreType.DMA((2,))],
        compiler_params=pltpu.CompilerParams(vmem_limit_bytes=WIDE),
        name="plan",
    )(block_utt, block_dest, frames, w_qkv.transpose(1, 0, 2), w_out.T, w_proj)


def unpack_kernel(gathered, main, proj, flat, stage):
    nz = gathered.shape[0] // PACKED
    for z in range(nz):
        flat[...] = gathered[z * PACKED : (z + 1) * PACKED, :].astype(F32)
        for i in range(TILES):
            stage[z * K_DEV : (z + 1) * K_DEV, i * 128 : (i + 1) * 128] = flat[
                i * K_DEV : (i + 1) * K_DEV, :
            ]
    main[...] = stage[:, :D].astype(BF16)
    proj[...] = stage[:, D:].astype(BF16)


def unpack_call(gathered):
    rows = gathered.shape[0] // PACKED * K_DEV
    return pl.pallas_call(
        unpack_kernel,
        out_shape=(
            jax.ShapeDtypeStruct((rows, D), BF16),
            jax.ShapeDtypeStruct((rows, PROJ), BF16),
        ),
        in_specs=[VMEM()],
        out_specs=(VMEM(), VMEM()),
        scratch_shapes=[
            pltpu.VMEM((PACKED, 128), F32),
            pltpu.VMEM((rows, D + PROJ), F32),
        ],
        compiler_params=pltpu.CompilerParams(vmem_limit_bytes=32 * MIB),
        cost_estimate=pl.CostEstimate(flops=0, bytes_accessed=2 * MIB, transcendentals=0),
        name="unpack",
    )(gathered)


def layer_norm(values, gain, shift):
    centre = jnp.mean(values, axis=-1, keepdims=True)
    centred = values - centre
    spread = jnp.mean(centred * centred, axis=-1, keepdims=True)
    return centred * lax.rsqrt(spread + EPS) * gain + shift


def split_exact(values):
    high = values.astype(BF16)
    rest = values - high.astype(F32)
    middle = rest.astype(BF16)
    low = (rest - middle.astype(F32)).astype(BF16)
    return [high, middle, low]


def parity_rows():
    rows = lax.broadcasted_iota(jnp.int32, (FRAMES, FRAMES), 0)
    cols = lax.broadcasted_iota(jnp.int32, (FRAMES, FRAMES), 1)
    picked = jnp.where(rows < HALF, 2 * rows, 2 * (rows - HALF) + 1)
    return jnp.where(cols == picked, 1.0, 0.0).astype(BF16)


def feature_select(start):
    feature = lax.broadcasted_iota(jnp.int32, (D, 256), 0)
    position = lax.broadcasted_iota(jnp.int32, (1, 256), 1) + start
    return jnp.where(feature == feature_at(position), 1.0, 0.0).astype(BF16)


def prepare_kernel(
    plan, frames, near, gain, shift, post_gain, post_shift,
    normed, residual, post, blocks, stack, sems,
):
    for g in range(CAP):
        source = plan[g]

        @pl.when((source >= 0) & (source < BLK_IN))
        def _():
            pltpu.make_async_copy(frames.at[source], blocks.at[g], sems.at[g]).start()

        @pl.when(source == BLK_IN + 1)
        def _():
            pltpu.make_async_copy(near, blocks.at[g], sems.at[g]).start()

        @pl.when((source < 0) | (source == BLK_IN))
        def _():
            blocks[g] = jnp.zeros((FRAMES, D), BF16)

    row = (1, D)
    gain, shift = gain[...].reshape(row), shift[...].reshape(row)
    parts = split_exact(post_gain[...].reshape(row))
    parts += split_exact(post_shift[...].reshape(row))
    stack[ROWS + FRAMES :, :] = jnp.concatenate(
        parts + [jnp.zeros((10, D), BF16)], axis=0
    )
    for g in range(CAP):

        @pl.when((plan[g] >= 0) & (plan[g] != BLK_IN))
        def _():
            pltpu.make_async_copy(near, blocks.at[g], sems.at[g]).wait()

    parity = parity_rows()
    for g in range(CAP):
        sorted_rows = jnp.dot(parity, blocks[g], preferred_element_type=F32)
        done = layer_norm(sorted_rows, gain, shift).astype(BF16)
        stack[g * HALF : (g + 1) * HALF, :] = done[:HALF]
        stack[POOLED + g * HALF : POOLED + (g + 1) * HALF, :] = done[HALF:]
    own = blocks[lax.axis_index("section")]
    stack[ROWS : ROWS + FRAMES, :] = jnp.dot(
        parity, own, preferred_element_type=F32
    ).astype(BF16)
    for start in range(0, D, 256):
        select = feature_select(start)
        moved = jnp.dot(stack[...], select, preferred_element_type=F32)
        span = slice(start, start + 256)
        normed[:, span] = moved[:ROWS].astype(BF16)
        residual[:, span] = 0.5 * (
            moved[ROWS : ROWS + HALF] + moved[ROWS + HALF : ROWS + FRAMES]
        )
        tail = moved[ROWS + FRAMES :]
        post[0:1, span] = tail[0:1] + (tail[1:2] + tail[2:3])
        post[1:2, span] = tail[3:4] + (tail[4:5] + tail[5:6])


def prepare_call(plan, frames, near, vectors):
    return pl.pallas_call(
        prepare_kernel,
        out_shape=(
            jax.ShapeDtypeStruct((ROWS, D), BF16),
            jax.ShapeDtypeStruct((HALF, D), F32),
            jax.ShapeDtypeStruct((2, D), F32),
        ),
        in_specs=[SMEM(), ANY(), ANY()] + [VMEM()] * 4,
        out_specs=(VMEM(), VMEM(), VMEM()),
        scratch_shapes=[
            pltpu.VMEM((CAP, FRAMES, D), BF16),
            pltpu.VMEM((ROWS + FRAMES + 16, D), BF16),
            pltpu.SemaphoreType.DMA((CAP,)),
        ],
        compiler_params=pltpu.CompilerParams(vmem_limit_bytes=24 * MIB),
        cost_estimate=pl.CostEstimate(
            flops=10**8, bytes_accessed=MIB, transcendentals=0
        ),
        name="prepare",
    )(plan, frames, near, *vectors)


def add_far_kernel(
    plan, far, gain, shift, normed_in, residual_in, normed, residual,
    stack, moved, pooled, sems,
):
    slot = jnp.int32(-1)
    for g in range(CAP):
        slot = jnp.where(plan[g] == BLK_IN, g, slot)
    own = slot == lax.axis_index("section")

    @pl.when(slot >= 0)
    def _():
        row = (1, D)
        placed = jnp.dot(parity_rows(), far[...], preferred_element_type=F32)
        done = layer_norm(placed, gain[...].reshape(row), shift[...].reshape(row))
        stack[:FRAMES, :] = done.astype(BF16)
        stack[FRAMES:, :] = placed.astype(BF16)
        for start in range(0, D, 256):
            span = slice(start, start + 256)
            out = jnp.dot(stack[...], feature_select(start), preferred_element_type=F32)
            moved[:, span] = out[:FRAMES].astype(BF16)
            pooled[:, span] = 0.5 * (out[FRAMES : FRAMES + HALF] + out[FRAMES + HALF :])
        copies = [
            pltpu.make_async_copy(
                moved.at[pl.ds(i * HALF, HALF)],
                normed.at[pl.ds(pl.multiple_of(i * POOLED + slot * HALF, HALF), HALF)],
                sems.at[i],
            )
            for i in range(2)
        ]
        for copy in copies:
            copy.start()

        @pl.when(own)
        def _():
            copy = pltpu.make_async_copy(pooled, residual, sems.at[2])
            copy.start()
            copy.wait()

        for copy in copies:
            copy.wait()


def add_far_call(plan, far, gain, shift, normed, residual):
    return pl.pallas_call(
        add_far_kernel,
        out_shape=(
            jax.ShapeDtypeStruct((ROWS, D), BF16),
            jax.ShapeDtypeStruct((HALF, D), F32),
        ),
        in_specs=[SMEM(), VMEM(), VMEM(), VMEM(), ANY(), ANY()],
        out_specs=(ANY(), ANY()),
        scratch_shapes=[
            pltpu.VMEM((2 * FRAMES, D), BF16),
            pltpu.VMEM((FRAMES, D), BF16),
            pltpu.VMEM((HALF, D), F32),
            pltpu.SemaphoreType.DMA((3,)),
        ],
        input_output_aliases={4: 0, 5: 1},
        compiler_params=pltpu.CompilerParams(vmem_limit_bytes=24 * MIB),
        cost_estimate=pl.CostEstimate(
            flops=10**8, bytes_accessed=MIB, transcendentals=0
        ),
        name="add_far",
    )(plan, far, gain, shift, normed, residual)


def attend_kernel(plan, normed, mine, other, terms):
    slot_row = lax.broadcasted_iota(jnp.int32, (ROWS, 1), 0) % POOLED // HALF
    slot_col = lax.broadcasted_iota(jnp.int32, (1, ROWS), 1) % POOLED // HALF
    owner_row = jnp.full((ROWS, 1), -1, jnp.int32)
    owner_col = jnp.full((1, ROWS), -1, jnp.int32)
    for g in range(CAP):
        owner = plan[CAP + g]
        owner_row = jnp.where(slot_row == g, owner, owner_row)
        owner_col = jnp.where(slot_col == g, owner, owner_col)
    same = owner_row == owner_col
    low = lax.broadcasted_iota(jnp.int32, (1, 128), 1) < HEAD
    left, right = normed[:, :HALF_D], normed[:, HALF_D:]

    def project(start, size):
        span = slice(start, start + size)
        return jnp.dot(left, mine[:, span], preferred_element_type=F32) + jnp.dot(
            right, other[:, span], preferred_element_type=F32
        )

    def head(query, keyed, valued, use_low):
        query = jnp.where(low == use_low, query * HEAD ** (-0.5), 0.0).astype(BF16)
        scores = lax.dot_general(query, keyed, NT, preferred_element_type=F32)
        scores = jnp.where(same, scores, NEG)
        peak = jnp.max(scores, axis=1, keepdims=True)
        weight = jnp.exp(scores - peak)
        total = jnp.sum(weight, axis=1, keepdims=True)
        out = jnp.dot(weight.astype(BF16), valued, preferred_element_type=F32)
        out = out * (0.5 / total)
        return out[:POOLED] + out[POOLED:]

    queries = project(0, 256)
    keys = project(256, 256).astype(BF16)
    values = project(512, 256).astype(BF16)
    tail = project(1024, 256)
    pieces = []
    for pair in range(2):
        span = slice(pair * 128, (pair + 1) * 128)
        query, keyed, valued = queries[:, span], keys[:, span], values[:, span]
        first = head(query, keyed, valued, True)
        second = head(query, keyed, valued, False)
        pieces.append(jnp.where(low, first, second).astype(BF16))
    pair = tail[:, :128]
    rolled = pltpu.roll(pair, HEAD, 1).astype(BF16)
    fifth = head(pair, rolled, tail[:, 128:].astype(BF16), True)
    fifth = pltpu.roll(fifth, HEAD, 1)
    fifth = jnp.where(low, 0.0, fifth).astype(BF16)
    pooled = jnp.concatenate(pieces + [fifth], axis=1)
    for side, weights in enumerate((mine, other)):
        for start in range(0, HALF_D, 128):
            rows = slice(start, start + 128)
            out = lax.dot_general(
                pooled[:, :256], weights[rows, 768:1024], NT, preferred_element_type=F32
            ) + lax.dot_general(
                pooled[:, 256:], weights[rows, 1152:1280], NT, preferred_element_type=F32
            )
            start += side * HALF_D
            terms[:, start : start + 128] = out.astype(BF16)


def attend_call(plan, normed, mine, other):
    return pl.pallas_call(
        attend_kernel,
        out_shape=jax.ShapeDtypeStruct((POOLED, D), BF16),
        in_specs=[SMEM(), VMEM(), VMEM(), VMEM()],
        out_specs=VMEM(),
        compiler_params=pltpu.CompilerParams(vmem_limit_bytes=24 * MIB),
        cost_estimate=pl.CostEstimate(
            flops=3 * 10**9, bytes_accessed=8 * MIB, transcendentals=5 * ROWS * ROWS
        ),
        name="attend",
    )(plan, normed, mine, other)


def finish_kernel(terms, residual, post, out):
    total = residual[...]
    for s in range(terms.shape[0] // HALF):
        total += terms[s * HALF : (s + 1) * HALF, :].astype(F32)
    out[...] = layer_norm(total, post[0:1, :], post[1:2, :]).astype(BF16)


def finish_call(terms, residual, post):
    return pl.pallas_call(
        finish_kernel,
        out_shape=jax.ShapeDtypeStruct((HALF, D), BF16),
        in_specs=[VMEM()] * 3,
        out_specs=VMEM(),
        compiler_params=pltpu.CompilerParams(vmem_limit_bytes=16 * MIB),
        name="finish",
    )(terms, residual, post)


def project_kernel(plan, rows, mine, other, bias, out):
    slot = lax.broadcasted_iota(jnp.int32, (POOLED, 1), 0) // HALF
    live = jnp.full((POOLED, 1), -1, jnp.int32)
    for g in range(CAP):
        live = jnp.where(slot == g, plan[CAP + g], live)
    left, right = rows[:, :HALF_D], rows[:, HALF_D:]
    for start in range(0, PROJ, 256):
        span = slice(start, start + 256)
        value = jnp.dot(left, mine[:, span], preferred_element_type=F32) + jnp.dot(
            right, other[:, span], preferred_element_type=F32
        )
        value = value + bias[:, span]
        out[:, span] = jnp.where(live >= 0, value, 0.0).astype(BF16)


def project_call(plan, rows, mine, other, bias):
    return pl.pallas_call(
        project_kernel,
        out_shape=jax.ShapeDtypeStruct((POOLED, PROJ), BF16),
        in_specs=[SMEM(), VMEM(), VMEM(), VMEM(), VMEM()],
        out_specs=VMEM(),
        compiler_params=pltpu.CompilerParams(vmem_limit_bytes=24 * MIB),
        cost_estimate=pl.CostEstimate(
            flops=2 * POOLED * D * PROJ, bytes_accessed=4 * MIB, transcendentals=0
        ),
        name="project",
    )(plan, rows, mine, other, bias)


def y_shift(slabs, steps):
    pairs = [
        ((y + (NY - steps if core else steps)) % NY * NC + core, y * NC + core)
        for y in range(NY)
        for core in range(NC)
    ]
    return lax.ppermute(slabs, ("y", "core"), pairs)


def other_core(slabs):
    return lax.ppermute(slabs, "core", [(0, 1), (1, 0)])


def shards(
    frames,
    block_utt,
    block_dest,
    ln_gain,
    ln_shift,
    w_qkv,
    w_out,
    post_gain,
    post_shift,
    w_proj,
    proj_bias,
):
    plan, packed, far, near = plan_call(
        block_utt, block_dest, frames, w_qkv, w_out, w_proj
    )
    gathered = lax.all_gather(packed, "z", axis=0, tiled=True)
    main, proj = unpack_call(gathered)
    main, far, near = lax.optimization_barrier((main, far, near))
    slabs = {steps: y_shift(main, steps) for steps in (2, 1, 3)}
    mine = jnp.concatenate([main, slabs[1], slabs[2], slabs[3]], axis=0)
    odd = range(1, lax.axis_size(DP) - 1, 2)
    far = lax.ppermute(far, DP, [(i, i + 1) for i in odd] + [(i + 1, i) for i in odd])
    near, proj = lax.optimization_barrier((other_core(near), proj))
    proj_pair = jnp.concatenate([proj, y_shift(proj, 1)], axis=0)
    vectors = (ln_gain, ln_shift, post_gain, post_shift)
    normed, residual, post = prepare_call(plan, frames, near, vectors)
    normed, residual = add_far_call(plan, far, ln_gain, ln_shift, normed, residual)
    mine, normed, proj_pair = lax.optimization_barrier((mine, normed, proj_pair))
    other = other_core(mine)
    proj_rest = y_shift(proj_pair, 2)
    terms = attend_call(plan, normed, mine, other)
    terms = lax.all_to_all(terms, "section", split_axis=0, concat_axis=0, tiled=True)
    pooled_norm = finish_call(terms, residual, post)
    pooled_norm, proj_pair, proj_rest = lax.optimization_barrier(
        (pooled_norm, proj_pair, proj_rest)
    )
    proj_mine = jnp.concatenate([proj_pair, proj_rest], axis=0)
    proj_other = other_core(proj_mine)
    rows = lax.all_gather(pooled_norm, "section", axis=0, tiled=True)
    bias = proj_bias.reshape(1, PROJ)
    lm_local = project_call(plan, rows, proj_mine, proj_other, bias)
    return lax.all_to_all(lm_local, "section", split_axis=0, concat_axis=1, tiled=True)


def solution(mesh):
    dp, section = mesh.devices.shape
    shape = (dp // (NY * NC), NY, NC, section)
    fine = Mesh(mesh.devices.reshape(shape), DP + ("section",))
    return jax.shard_map(
        shards,
        mesh=fine,
        in_specs=(
            P(DP, None, None),
            P(),
            P(),
            P(),
            P(),
            P(None, DP, "section"),
            P("section", DP),
            P(),
            P(),
            P(DP, "section"),
            P("section"),
        ),
        out_specs=P(DP + ("section",), None),
        check_vma=False,
    )
```
